128 devices in a mesh: gx: 16 (over y_lo, z, core), gy: 8 (over y_hi, x).
Axes of the slice: x: 4, y: 4 (y_hi: 2, y_lo: 2; y = y_hi * 2 + y_lo), z: 4, core: 2. Of those that a mesh axis runs over, the one named last changes fastest.
Arguments:
- e_field: float32 [3, 64, 64, 1024], P(None, None, 'gx', 'gy'), may hold values from -6 to 6
- h_field: float32 [3, 64, 64, 1024], P(None, None, 'gx', 'gy'), may hold values from -6 to 6
- drude_current: float32 [3, 64, 64, 1024], P(None, None, 'gx', 'gy'), may hold values from -6 to 6
- lorentz_polar: float32 [3, 64, 64, 1024], P(None, None, 'gx', 'gy'), may hold values from -6 to 6
- lorentz_rate: float32 [3, 64, 64, 1024], P(None, None, 'gx', 'gy'), may hold values from -6 to 6
- permittivity: float32 [64, 64, 1024], P(None, 'gx', 'gy'), may hold values from 1 to 6
- material: int32 [64, 64, 1024], P(None, 'gx', 'gy'), may hold values from 0 to 2
- absorber: int32 [64, 64, 1024], P(None, 'gx', 'gy'), may hold values from 0 to 3
Outputs:
- e_out: float32 [3, 64, 64, 1024], P(None, None, 'gx', 'gy')
- h_out: float32 [3, 64, 64, 1024], P(None, None, 'gx', 'gy')
The draws below stay inside these ranges and needn't reach their ends.
All inputs are finite; a program needn't handle non-finite values.
Results may differ from the reference program's by a relative error of at most 0.00002.
Values sent between devices are 32-bit elements; how exact they have to be, the bound alone decides.
A program may use at most 64 MiB of HBM per device.

```python
import math
import jax
import jax.numpy as jnp

NZ = 64
STEPS = 14
NX = 64
NY = 1024


def touch_ends(entries, rng, least, largest):
    place = [jax.random.randint(jax.random.fold_in(rng, axis), (), 0, length) for axis, length in enumerate(entries.shape)]
    longest = entries.shape.index(max(entries.shape))
    beside = place[:longest] + [(place[longest] + 1) % entries.shape[longest]] + place[longest + 1:]
    return entries.at[tuple(place)].set(least).at[tuple(beside)].set(largest)


def shard_levels(rng, shape, cuts, least, largest):
    gain, own = 1.0, jax.random.fold_in(rng, 6)
    for position, shards_of in cuts:
        steps = jnp.exp(jax.random.uniform(jax.random.fold_in(own, position), (shards_of,), jnp.float32, least / len(cuts), largest / len(cuts)))
        gain = gain * jnp.repeat(steps, shape[position] // shards_of).reshape([-1 if axis == position else 1 for axis in range(len(shape))])
    return gain


def scatter_about(stream_key, shape, deviation, limit, split=(), held_as=jnp.bfloat16):
    factor_of = shard_levels(stream_key, shape, split, -0.22, 0.18) if split else 1.0
    entries = jax.random.normal(stream_key, shape, jnp.float32) * deviation * factor_of
    return jnp.minimum(jnp.maximum(entries, -limit), limit).astype(held_as)


def setup_inputs(seed: int = 0) -> dict:
    streams_of = jax.random.split(jax.random.key(seed), 9)
    e_field = scatter_about(streams_of[0], (3, NZ, NX, NY), 1.0, 6.0, ((2, 16), (3, 8)), jnp.float32)
    h_field = scatter_about(streams_of[1], (3, NZ, NX, NY), 1.0, 6.0, ((2, 16), (3, 8)), jnp.float32)
    drude_current = scatter_about(streams_of[2], (3, NZ, NX, NY), 1.0, 6.0, ((2, 16), (3, 8)), jnp.float32)
    lorentz_polar = scatter_about(streams_of[3], (3, NZ, NX, NY), 1.0, 6.0, ((2, 16), (3, 8)), jnp.float32)
    lorentz_rate = scatter_about(streams_of[4], (3, NZ, NX, NY), 1.0, 6.0, ((2, 16), (3, 8)), jnp.float32)
    permittivity = jnp.clip(jnp.exp(math.log(6.0) - 1.7917595 * jax.random.uniform(streams_of[5], (NZ, NX, NY), jnp.float32) ** shard_levels(streams_of[5], (NZ, NX, NY), ((1, 16), (2, 8)), -0.2, 0.2)), 1.0, 6.0)
    material = touch_ends(jax.random.randint(streams_of[6], (NZ, NX, NY), 0, 3), jax.random.fold_in(streams_of[6], 1), 0, 2).astype(jnp.int32)
    absorber = touch_ends(jax.random.randint(streams_of[7], (NZ, NX, NY), 0, 4), jax.random.fold_in(streams_of[7], 1), 0, 3).astype(jnp.int32)
    return {"e_field": e_field, "h_field": h_field, "drude_current": drude_current, "lorentz_polar": lorentz_polar, "lorentz_rate": lorentz_rate, "permittivity": permittivity, "material": material, "absorber": absorber}


def coefficients(absorber, material, permittivity):
    s = 0.1 * absorber.astype(jnp.float32)
    eff = jnp.where(material == 0, jnp.float32(1.0), permittivity)
    metal = jnp.where(material == 2, jnp.float32(1.0), jnp.float32(0.0))
    ah = (1.0 - s) / (1.0 + s)
    bh = 0.5 / (1.0 + s)
    se = s / eff
    ae = (1.0 - se) / (1.0 + se)
    be = 0.5 / (eff * (1.0 + se))
    return ah, bh, ae, be, metal


def up_z(comp):
    return jnp.concatenate([comp[1:], jnp.zeros_like(comp[:1])], 0)


def low_z(comp):
    return jnp.concatenate([jnp.zeros_like(comp[:1]), comp[:-1]], 0)


def curl_e(e, ux_y, ux_z, uy_x, uy_z):
    ex, ey, ez = e[0], e[1], e[2]
    cx = (uy_z - ez) - (up_z(ey) - ey)
    cy = (up_z(ex) - ex) - (ux_z - ez)
    cz = (ux_y - ey) - (uy_x - ex)
    return jnp.stack([cx, cy, cz])


def curl_h(h, lx_y, lx_z, ly_x, ly_z):
    hx, hy, hz = h[0], h[1], h[2]
    cx = (hz - ly_z) - (hy - low_z(hy))
    cy = (hx - low_z(hx)) - (hz - lx_z)
    cz = (hy - lx_y) - (hx - ly_x)
    return jnp.stack([cx, cy, cz])


def media(e, drude, polar, rate):
    drude = (0.975 / 1.025) * drude + (1.125 / 1.025) * e
    rate = rate + 0.5 * (e - polar - 0.2 * rate)
    polar = polar + 0.5 * rate
    return drude, polar, rate


def reference(e_field, h_field, drude_current, lorentz_polar, lorentz_rate, permittivity, material, absorber):
    ah, bh, ae, be, metal = coefficients(absorber, material, permittivity)
    e, h = e_field, h_field
    drude, polar, rate = drude_current, lorentz_polar, lorentz_rate
    for step in range(STEPS):
        curl = curl_e(e, jnp.roll(e[1], -1, 1), jnp.roll(e[2], -1, 1), jnp.roll(e[0], -1, 2), jnp.roll(e[2], -1, 2))
        h = ah * h - bh * curl
        drude, polar, rate = media(e, drude, polar, rate)
        back = curl_h(h, jnp.roll(h[1], 1, 1), jnp.roll(h[2], 1, 1), jnp.roll(h[0], 1, 2), jnp.roll(h[2], 1, 2))
        e = ae * e + be * (back - metal * (drude + rate))
    return e, h
```

```python
import jax
import jax.numpy as jnp
from jax import lax
from jax.experimental import pallas as pl
from jax.experimental.pallas import tpu as pltpu
from jax.sharding import PartitionSpec as P

STEPS = 14
BLOCKS = 4
MESH = pl.DeviceIdType.MESH

ROWS = 80
TOP = 8
TALL = 96
TILES = ROWS // 8
OWN = 2
CROSS = 8
ZERO_H = 9
FREE = 10
ZERO_E = 14
PLANES = 15

C_J = 0.975 / 1.025
C_E = 2.0 * (1.125 / 1.025)


def towards(axis, step):
    count = lax.axis_size(axis)
    return {axis: lax.rem(lax.axis_index(axis) + step + count, count)}


def lanes():
    return lax.broadcasted_iota(jnp.int32, (8, 128), 1)


def pipelined(load, work):
    loaded = load(0)
    for t in range(TILES):
        later = load(t + 1) if t + 1 < TILES else None
        work(t, loaded)
        loaded = later


def h_pass(e, h, ah, bh, src, nxt, dst, cell):
    last = lax.rem(lanes(), 64) == 63

    def load(t):
        r = TOP + 8 * t
        here, beside = pl.ds(r, 8), pl.ds(r + 1, 8)
        return (
            e[0, src, here], e[1, src, here], e[2, src, here],
            e[0, src, beside], e[2, src, beside],
            e[1, nxt, here], e[2, nxt, here],
            h[0, src, here], h[1, src, here], h[2, src, here],
            ah[cell, pl.ds(8 * t, 8)], bh[cell, pl.ds(8 * t, 8)],
        )

    def work(t, loaded):
        ex, ey, ez, ex_y, ez_y, ey_x, ez_x, hx, hy, hz, a, b = loaded
        ex_z = jnp.where(last, 0.0, pltpu.roll(ex, 127, 1))
        ey_z = jnp.where(last, 0.0, pltpu.roll(ey, 127, 1))
        here = pl.ds(TOP + 8 * t, 8)
        h[0, dst, here] = a * hx - b * ((ez_y - ez) - (ey_z - ey))
        h[1, dst, here] = a * hy - b * ((ex_z - ex) - (ez_x - ez))
        h[2, dst, here] = a * hz - b * ((ey_x - ey) - (ex_y - ex))

    pipelined(load, work)
    for c in (0, 2):
        h[c, dst, pl.ds(TOP - 1, 1)] = pltpu.roll(h[c, dst, pl.ds(TOP + ROWS - 1, 1)], 64, 1)


def e_pass(e, h, j, p, q, ae, be, bm, src, mag, prv, dst, cell):
    first = lax.rem(lanes(), 64) == 0

    def load(t):
        r = TOP + 8 * t
        here, beside = pl.ds(r, 8), pl.ds(r - 1, 8)
        media = tuple((e[c, src, here], j[c, src, here], p[c, src, here], q[c, src, here]) for c in range(3))
        return media, (
            h[0, mag, here], h[1, mag, here], h[2, mag, here],
            h[0, mag, beside], h[2, mag, beside],
            h[1, prv, here], h[2, prv, here],
            ae[cell, pl.ds(8 * t, 8)], be[cell, pl.ds(8 * t, 8)], bm[cell, pl.ds(8 * t, 8)],
        )

    def work(t, loaded):
        media, (hx, hy, hz, hx_y, hz_y, hy_x, hz_x, a, b, m) = loaded
        hx_z = jnp.where(first, 0.0, pltpu.roll(hx, 1, 1))
        hy_z = jnp.where(first, 0.0, pltpu.roll(hy, 1, 1))
        curl = (
            (hz - hz_y) - (hy - hy_z),
            (hx - hx_z) - (hz - hz_x),
            (hy - hy_x) - (hx - hx_y),
        )
        here = pl.ds(TOP + 8 * t, 8)
        for c in range(3):
            ec, jc, pc, qc = media[c]
            jc = C_J * jc + C_E * ec
            qc = 0.9 * qc + (ec - pc)
            pc = pc + 0.25 * qc
            j[c, dst, here] = jc
            q[c, dst, here] = qc
            p[c, dst, here] = pc
            e[c, dst, here] = a * ec + (b * curl[c] - m * (jc + qc))

    pipelined(load, work)
    for c in (0, 2):
        seam_e(e, c, dst)


def seam_e(e, c, plane):
    e[c, plane, pl.ds(TOP + ROWS, 1)] = pltpu.roll(e[c, plane, pl.ds(TOP, 1)], 64, 1)


def kernel(
    e_in, h_in, j_in, p_in, q_in, perm_in, mat_in, abs_in, e_out, h_out,
    stage, ints, tall, tall_c, e, h, j, p, q, ah, bh, ae, be, bm,
    send_e, send_h, recv_e, recv_h, in_sem, y_sem, x_sem, se_sem, re_sem, sh_sem, rh_sem,
):
    barrier = pltpu.get_barrier_semaphore()
    for axis in ("gx", "gy"):
        for step in (-1, 1):
            pl.semaphore_signal(barrier, inc=1, device_id=towards(axis, step), device_id_type=MESH)

    fields = (e_in, h_in, j_in, p_in, q_in)
    loads = [pltpu.make_async_copy(f, stage.at[pl.ds(3 * i, 3)], in_sem.at[i]) for i, f in enumerate(fields)]
    loads.append(pltpu.make_async_copy(perm_in, stage.at[15], in_sem.at[5]))
    loads.append(pltpu.make_async_copy(mat_in, ints.at[0], in_sem.at[6]))
    loads.append(pltpu.make_async_copy(abs_in, ints.at[1], in_sem.at[7]))
    for load in loads:
        load.start()

    def clear(planes, refs):
        def body(i, carry):
            for ref in refs:
                for plane in planes:
                    for c in range(3):
                        ref[c, plane, pl.ds(pl.multiple_of(8 * i, 8), 8)] = jnp.zeros((8, 128), jnp.float32)
            return carry

        lax.fori_loop(0, TALL // 8, body, 0)

    clear((ZERO_E,), (e,))
    clear((ZERO_H,), (h,))

    for load in loads:
        load.wait()

    def turn(first, second, out):
        out[pl.ds(16, 128)] = jnp.transpose(jnp.concatenate([first, second], 0))

    def turn_field(i, carry):
        for pair in range(2):
            rows = [stage[i, pl.ds(2 * pair + k, 64, stride=4)] for k in range(2)]
            turn(rows[0], rows[1], tall.at[2 * i + pair])
        return carry

    lax.fori_loop(0, 15, turn_field, 0)
    for pair in range(2):
        rows = [stage[15, pl.ds(2 * pair + k, 64, stride=4)] for k in range(2)]
        turn(rows[0], rows[1], tall_c.at[1 + pair, 0])
        for i in range(2):
            rows = [ints[i, pl.ds(2 * pair + k, 64, stride=4)].astype(jnp.float32) for k in range(2)]
            turn(rows[0], rows[1], tall_c.at[1 + pair, 1 + i])

    pl.semaphore_wait(barrier, 4)

    def columns(ref, k, step, k0):
        source, target = (pl.ds(16, 16), pl.ds(144, 16)) if step < 0 else (pl.ds(128, 16), pl.ds(0, 16))
        if k == 0:
            src, dst = ref.at[:, source], ref.at[:, target]
        else:
            src, dst = ref.at[pl.ds(1, 2), :, source], ref.at[pl.ds(1, 2), :, target]
        return pltpu.make_async_remote_copy(
            src_ref=src, dst_ref=dst, send_sem=y_sem.at[0, k0], recv_sem=y_sem.at[1, k0],
            device_id=towards("gy", step), device_id_type=MESH,
        )

    ghosts = [columns(tall_c, 1, -1, 0), columns(tall_c, 1, 1, 1), columns(tall, 0, -1, 2), columns(tall, 0, 1, 3)]
    for copy in ghosts:
        copy.start()
    for copy in ghosts[:2]:
        copy.wait()

    def planes(step):
        source, target = (1, 3) if step < 0 else (2, 0)
        k = 0 if step < 0 else 1
        return pltpu.make_async_remote_copy(
            src_ref=tall_c.at[source], dst_ref=tall_c.at[target],
            send_sem=x_sem.at[0, k], recv_sem=x_sem.at[1, k],
            device_id=towards("gx", step), device_id_type=MESH,
        )

    layers = [planes(-1), planes(1)]
    for copy in layers:
        copy.start()

    low = lanes() < 64

    def halves(ref, t):
        lower, upper = ref[pl.ds(8 * t, 8)], ref[pl.ds(ROWS + 8 * t, 8)]
        return (
            jnp.where(low, lower, pltpu.roll(upper, 64, 1)),
            jnp.where(low, pltpu.roll(lower, 64, 1), upper),
        )

    def coefficients(group):
        for t in range(TILES):
            raw = [halves(tall_c.at[group, i], t) for i in range(3)]
            here = pl.ds(8 * t, 8)
            for k in range(2):
                perm, mat, absorb = raw[0][k], raw[1][k], raw[2][k]
                s = 0.1 * absorb
                eff = jnp.where(mat == 0.0, 1.0, perm)
                plane = 2 * group + k
                r = 1.0 / (1.0 + s)
                ah[plane, here] = (1.0 - s) * r
                bh[plane, here] = 0.5 * r
                se = s / eff
                r = 1.0 / (1.0 + se)
                ae[plane, here] = (1.0 - se) * r
                b = 0.5 * r / eff
                be[plane, here] = b
                bm[plane, here] = jnp.where(mat == 2.0, 0.5 * b, 0.0)

    lax.fori_loop(1, 3, lambda g, carry: (coefficients(g), carry)[1], 0)

    for copy in ghosts[2:]:
        copy.wait()

    def build(ref, f, scale):
        def body(i, carry):
            c, pair = i // 2, lax.rem(i, 2)
            for t in range(TILES):
                first, second = halves(tall.at[6 * f + i], t)
                here = pl.ds(TOP + 8 * t, 8)
                ref[c, OWN + 2 * pair, here] = first * scale if scale != 1 else first
                ref[c, OWN + 1 + 2 * pair, here] = second * scale if scale != 1 else second
            return carry

        lax.fori_loop(0, 6, body, 0)

    build(e, 0, 1)
    build(h, 1, 1)
    build(j, 2, 2.0)
    build(p, 3, 1)
    build(q, 4, 2.0)
    for x in range(4):
        for c in (0, 2):
            seam_e(e, c, OWN + x)

    def trace_e(step):
        return pltpu.make_async_remote_copy(
            src_ref=send_e.at[step], dst_ref=recv_e.at[step],
            send_sem=se_sem.at[step], recv_sem=re_sem.at[step],
            device_id=towards("gx", -1), device_id_type=MESH,
        )

    def trace_h(step):
        return pltpu.make_async_remote_copy(
            src_ref=send_h.at[step], dst_ref=recv_h.at[step],
            send_sem=sh_sem.at[step], recv_sem=rh_sem.at[step],
            device_id=towards("gx", 1), device_id_type=MESH,
        )

    def give(ref, plane, out, step):
        for c in range(2):
            for t in range(TILES):
                out[step, c, pl.ds(8 * t, 8)] = ref[1 + c, plane, pl.ds(TOP + 8 * t, 8)]

    def take(ref, plane, trace, step):
        for c in range(2):
            for t in range(TILES):
                here = pl.ds(TOP + 8 * t, 8)
                ref[1 + c, CROSS, here] = ref[1 + c, plane, here] + trace[step, c, pl.ds(8 * t, 8)]

    def loop(low, high, body):
        lax.fori_loop(low, high, lambda i, carry: (body(i), carry)[1], 0)

    def block(b, carry):
        size = 4 - b // 2
        start = 4 * b - b // 3

        def free(i):
            more = (i + 3) // 4
            base = OWN + more * (FREE - OWN)
            give(e, base, send_e, start + i)
            trace_e(start + i).start()
            final = (i + 1) // size

            def free_h(x):
                nxt = base + x + 1 + (x // 3) * (ZERO_E - base - 4)
                h_pass(e, h, ah, bh, base + x, nxt, FREE + x, OWN + x)

            loop(3 * final, 4, free_h)
            give(h, FREE + 3, send_h, start + i)
            trace_h(start + i).start()

            def free_e(x):
                e_pass(e, h, j, p, q, ae, be, bm, base + x, FREE + x, FREE + x - 1, FREE + x, OWN + x)

            loop(4 * final, 4, free_e)

        loop(0, size, free)

        clear((0, 1, 6, 7), (e, h, j, p, q))

        def ghost_coefficients(i):
            for copy in layers:
                copy.wait()
            coefficients(0)
            coefficients(3)

        loop(0, 1 - (b + 3) // 4, ghost_coefficients)

        def true(i):
            step = start + i
            first = 1 - (i + 3) // 4
            final = (i + 1) // size
            edge = first + final
            deep = ((i + 3) // 4) * (1 - (i + 2) // size)

            loop(edge, 5, lambda x: h_pass(e, h, ah, bh, x, x + 1, x, x))
            trace_e(step).wait_recv()
            take(e, 6, recv_e, step)
            loop(5, 7 - edge, lambda x: h_pass(e, h, ah, bh, x, x + 1 + 2 * (1 - x // 6), x, x))

            ghost = 1 - final
            top = 6 + ghost + deep
            loop(3, top, lambda x: e_pass(e, h, j, p, q, ae, be, bm, x, x, x - 1, x, x))
            trace_h(step).wait_recv()
            take(h, 1, recv_h, step)

            def bottom(x):
                prv = x - 1 + 10 * (1 - (x + 1) // 2) + 7 * (x // 2)
                e_pass(e, h, j, p, q, ae, be, bm, x, x, prv, x, x)

            loop(2 - ghost - deep, 3, bottom)

        loop(0, size, true)
        return carry

    lax.fori_loop(0, BLOCKS, block, 0)

    def finish(step):
        trace_e(step).wait_send()
        trace_h(step).wait_send()

    loop(0, STEPS, finish)

    def unturn(ref, i):
        c, pair = i // 2, lax.rem(i, 2)
        first, second = OWN + 2 * pair, OWN + 2 * pair + 1
        wide = lax.broadcasted_iota(jnp.int32, (64, 128), 1) < 64
        up, down = pl.ds(TOP + 16, 64), pl.ds(TOP, 64)
        lower = jnp.where(wide, ref[c, first, up], pltpu.roll(ref[c, second, up], 64, 1))
        upper = jnp.where(wide, pltpu.roll(ref[c, first, down], 64, 1), ref[c, second, down])
        return jnp.transpose(jnp.concatenate([lower, upper], 0))

    for f, (ref, out) in enumerate(((e, e_out), (h, h_out))):
        def body(c):
            for pair in range(2):
                whole = unturn(ref, 2 * c + pair)
                stage[3 * f + c, pl.ds(2 * pair, 64, stride=4)] = whole[:64]
                stage[3 * f + c, pl.ds(2 * pair + 1, 64, stride=4)] = whole[64:]

        loop(0, 3, body)
        pltpu.make_async_copy(stage.at[pl.ds(3 * f, 3)], out, in_sem.at[f]).start()
    for f, out in enumerate((e_out, h_out)):
        pltpu.make_async_copy(stage.at[pl.ds(3 * f, 3)], out, in_sem.at[f]).wait()


def shards(
    e_field, h_field, drude_current, lorentz_polar, lorentz_rate, permittivity, material, absorber
):
    fields = [f.reshape(3, 256, 128) for f in (e_field, h_field, drude_current, lorentz_polar, lorentz_rate)]
    cells = [c.reshape(256, 128) for c in (permittivity, material, absorber)]
    f32 = jnp.float32
    state = pltpu.VMEM((3, PLANES, TALL, 128), f32)
    cell = pltpu.VMEM((8, ROWS, 128), f32)
    trace = pltpu.VMEM((STEPS, 2, ROWS, 128), f32)
    out = jax.ShapeDtypeStruct((3, 256, 128), f32)
    e, h = pl.pallas_call(
        kernel,
        out_shape=(out, out),
        in_specs=[pl.BlockSpec(memory_space=pl.ANY)] * 8,
        out_specs=(pl.BlockSpec(memory_space=pl.ANY),) * 2,
        scratch_shapes=[
            pltpu.VMEM((16, 256, 128), f32),
            pltpu.VMEM((2, 256, 128), jnp.int32),
            pltpu.VMEM((30, 160, 128), f32),
            pltpu.VMEM((4, 3, 160, 128), f32),
            state, state, state, state, state,
            cell, cell, cell, cell, cell,
            trace, trace, trace, trace,
            pltpu.SemaphoreType.DMA((8,)),
            pltpu.SemaphoreType.DMA((2, 4)),
            pltpu.SemaphoreType.DMA((2, 2)),
            pltpu.SemaphoreType.DMA((STEPS,)),
            pltpu.SemaphoreType.DMA((STEPS,)),
            pltpu.SemaphoreType.DMA((STEPS,)),
            pltpu.SemaphoreType.DMA((STEPS,)),
        ],
        compiler_params=pltpu.CompilerParams(
            collective_id=0, has_side_effects=True, vmem_limit_bytes=48 * 1024 * 1024
        ),
    )(*fields, *cells)
    return e.reshape(3, 64, 4, 128), h.reshape(3, 64, 4, 128)


def solution(mesh):
    field, cell = P(None, None, "gx", "gy"), P(None, "gx", "gy")
    return jax.shard_map(
        shards, mesh=mesh, in_specs=(field,) * 5 + (cell,) * 3, out_specs=(field, field), check_vma=False
    )
```

```python
import contextlib

import jax
import jax.numpy as jnp
from jax import lax
from jax.experimental import pallas as pl
from jax.experimental.pallas import tpu as pltpu
from jax.sharding import PartitionSpec as P

STEPS = 14
BLOCKS = 4
MESH = pl.DeviceIdType.MESH
NAMED = False
F32 = jnp.float32

TILES = 10
TILE = 16
COMP = 12 * TILE
ROWS = 80
OWN = 2
CROSS = 8
ZERO_H = 9
FREE = 10
ZERO_E = 14
PLANES = 15

C_J = 0.975 / 1.025
C_E = 2.0 * (1.125 / 1.025)

SLOTS = ["perm", "mat", "abs", "e0", "e1", "e2", "h0", "h1", "h2", "j0", "j1", "j2", "p0", "p1", "p2", "q0", "q1", "q2"]
GROUPS = 5


def scope(name):
    return jax.named_scope(name) if NAMED else contextlib.nullcontext()


def towards(axis, step):
    count = lax.axis_size(axis)
    return {axis: lax.rem(lax.axis_index(axis) + step + count, count)}


def lanes(rows=8):
    return lax.broadcasted_iota(jnp.int32, (rows, 128), 1)


def loop(low, high, body):
    lax.fori_loop(low, high, lambda i, carry: (body(i), carry)[1], 0)


def at(c, t, shift=0):
    return pl.ds(COMP * c + TILE * (t + 1) + shift, 8)


def packed(c, t):
    return pl.ds(ROWS * c + 8 * t, 8)


class Tiles:
    def __init__(self, ref, plane):
        self.ref, self.plane, self.held = ref, plane, {}

    def __call__(self, c, t):
        if (c, t) not in self.held:
            self.held[c, t] = self.ref[self.plane, at(c, t)]
        return self.held[c, t]


def pipelined(load, work):
    loaded = load(0)
    for t in range(TILES):
        later = load(t + 1) if t + 1 < TILES else None
        work(t, loaded)
        loaded = later


def h_pass(e, h, ah, bh, src, nxt, dst, cell):
    tile = Tiles(e, src)

    def load(t):
        here = pl.ds(8 * t, 8)
        return (
            [tile(c, t) for c in range(3)],
            tile(0, t + 1), tile(2, t + 1),
            e[src, at(0, t, 1)], e[src, at(1, t, 1)],
            e[nxt, at(1, t)], e[nxt, at(2, t)],
            [h[src, at(c, t)] for c in range(3)],
            ah[cell, here], bh[cell, here],
        )

    def work(t, loaded):
        (ex, ey, ez), ex_y, ez_y, ex_z, ey_z, ey_x, ez_x, (hx, hy, hz), a, b = loaded
        h[dst, at(0, t)] = a * hx - b * ((ez_y - ez) - (ey_z - ey))
        h[dst, at(1, t)] = a * hy - b * ((ex_z - ex) - (ez_x - ez))
        h[dst, at(2, t)] = a * hz - b * ((ey_x - ey) - (ex_y - ex))

    pipelined(load, work)


def e_pass(e, h, j, p, q, ae, be, bm, src, mag, prv, dst, cell):
    tile = Tiles(h, mag)

    def load(t):
        here = pl.ds(8 * t, 8)
        media = [(e[src, at(c, t)], j[src, packed(c, t)], p[src, packed(c, t)], q[src, packed(c, t)]) for c in range(3)]
        return (
            media,
            [tile(c, t) for c in range(3)],
            tile(0, t - 1), tile(2, t - 1),
            h[mag, at(0, t, -1)], h[mag, at(1, t, -1)],
            h[prv, at(1, t)], h[prv, at(2, t)],
            ae[cell, here], be[cell, here], bm[cell, here],
        )

    def work(t, loaded):
        media, (hx, hy, hz), hx_y, hz_y, hx_z, hy_z, hy_x, hz_x, a, b, m = loaded
        curl = (
            (hz - hz_y) - (hy - hy_z),
            (hx - hx_z) - (hz - hz_x),
            (hy - hy_x) - (hx - hx_y),
        )
        for c in range(3):
            ec, jc, pc, qc = media[c]
            jc = C_J * jc + C_E * ec
            qc = 0.9 * qc + (ec - pc)
            pc = pc + 0.25 * qc
            j[dst, packed(c, t)] = jc
            q[dst, packed(c, t)] = qc
            p[dst, packed(c, t)] = pc
            e[dst, at(c, t)] = a * ec + (b * curl[c] - m * (jc + qc))

    pipelined(load, work)


def edges_e(e, plane):
    tiles = [e[plane, at(c, 0)] for c in (0, 2)]
    first = e[plane, pl.ds(0, 24, stride=TILE)]
    tiles = [pltpu.roll(tile, 127, 1) for tile in tiles]
    first = jnp.where(lanes(24) < 112, pltpu.roll(first, 112, 1), 0.0)

    def store():
        e[plane, at(0, TILES)], e[plane, at(2, TILES)] = tiles
        e[plane, pl.ds(8, 24, stride=TILE)] = first

    return store


def edges_h(h, plane):
    tiles = [h[plane, at(c, TILES - 1)] for c in (0, 2)]
    last = h[plane, pl.ds(TILE + 7, 24, stride=TILE)]
    tiles = [pltpu.roll(tile, 1, 1) for tile in tiles]
    last = jnp.where(lanes(24) < 16, 0.0, pltpu.roll(last, 16, 1))

    def store():
        h[plane, at(0, -1)], h[plane, at(2, -1)] = tiles
        h[plane, pl.ds(TILE - 1, 24, stride=TILE)] = last

    return store


def kernel(
    e_in, h_in, j_in, p_in, q_in, perm_in, mat_in, abs_in, e_out, h_out,
    stage, ints, turned, raw, e, h, j, p, q, ah, bh, ae, be, bm,
    send_e, send_h, recv_e, recv_h, in_sem, y_sem, x_sem, se_sem, re_sem, sh_sem, rh_sem,
):
    barrier = pltpu.get_barrier_semaphore()
    for axis in ("gx", "gy"):
        for step in (-1, 1):
            pl.semaphore_signal(barrier, inc=1, device_id=towards(axis, step), device_id_type=MESH)

    fields = (e_in, h_in, j_in, p_in, q_in)
    loads = {
        "perm": pltpu.make_async_copy(perm_in, stage.at[0], in_sem.at[5]),
        "mat": pltpu.make_async_copy(mat_in, ints.at[0], in_sem.at[6]),
        "abs": pltpu.make_async_copy(abs_in, ints.at[1], in_sem.at[7]),
    }
    for i, f in enumerate(fields):
        loads["ehjpq"[i]] = pltpu.make_async_copy(f, stage.at[pl.ds(3 + 3 * i, 3)], in_sem.at[i])
    for load in loads.values():
        load.start()

    def clear(planes, refs):
        for ref in refs:
            size = ref.shape[1] // 6

            def body(i):
                for plane in planes:
                    for k in range(size // 8):
                        ref[plane, pl.ds(pl.multiple_of(size * i + 8 * k, 8), 8)] = jnp.zeros((8, 128), F32)

            loop(0, 6, body)

    clear((ZERO_E,), (e,))
    clear((ZERO_H,), (h,))

    def turn(g):
        def body(zb):
            rows = []
            for s in range(4):
                slot = 4 * g + s
                for x in range(4):
                    here = pl.ds(x, 8, stride=4)
                    if slot in (1, 2):
                        rows.append(ints[slot - 1, zb, here].astype(F32))
                    else:
                        rows.append(stage[min(slot, 17), zb, here])
            turned[g, zb, pl.ds(16, 128)] = jnp.transpose(jnp.concatenate(rows, 0))

        loop(0, 8, body)

    def columns(g, step):
        source, target = (pl.ds(16, 16), pl.ds(144, 16)) if step < 0 else (pl.ds(128, 16), pl.ds(0, 16))
        k = 2 * g + (step + 1) // 2
        return pltpu.make_async_remote_copy(
            src_ref=turned.at[g, :, source], dst_ref=turned.at[g, :, target],
            send_sem=y_sem.at[0, k], recv_sem=y_sem.at[1, k],
            device_id=towards("gy", step), device_id_type=MESH,
        )

    waited = set()
    for g in range(GROUPS):
        with scope("turn"):
            for name in SLOTS[4 * g : 4 * g + 4]:
                name = name if name in loads else name[0]
                if name not in waited:
                    waited.add(name)
                    loads[name].wait()
            turn(g)
        if g == 0:
            with scope("barrier"):
                pl.semaphore_wait(barrier, 4)
        for step in (-1, 1):
            columns(g, step).start()

    state = {"e": e, "h": h, "j": j, "p": p, "q": q}

    def build(g):
        def body(t):
            rows = [turned[g, zb, pl.ds(t, 16, stride=10)] for zb in range(8)]
            whole = jnp.transpose(jnp.concatenate(rows, 0))
            for s, name in enumerate(SLOTS[4 * g : 4 * g + 4]):
                for x in range(4):
                    part = whole[32 * s + 8 * x : 32 * s + 8 * x + 8]
                    if 4 * g + s < 3:
                        raw[OWN + x, 4 * g + s, pl.ds(pl.multiple_of(8 * t, 8), 8)] = part
                        continue
                    c = int(name[1])
                    if name[0] in "eh":
                        row = COMP * c + TILE * (t + 1)
                    else:
                        row = ROWS * c + 8 * t
                    if name[0] in "jq":
                        part = part * 2.0
                    state[name[0]][OWN + x, pl.ds(pl.multiple_of(row, 8), 8)] = part

        loop(0, TILES, body)

    def layers(step):
        source, target = (OWN, OWN + 4) if step < 0 else (OWN + 2, OWN - 2)
        k = (step + 1) // 2
        return pltpu.make_async_remote_copy(
            src_ref=raw.at[pl.ds(source, 2)], dst_ref=raw.at[pl.ds(target, 2)],
            send_sem=x_sem.at[0, k], recv_sem=x_sem.at[1, k],
            device_id=towards("gx", step), device_id_type=MESH,
        )

    def coefficients(plane):
        for t in range(TILES):
            here = pl.ds(8 * t, 8)
            perm, mat, absorb = (raw[plane, i, here] for i in range(3))
            s = 0.1 * absorb
            eff = jnp.where(mat == 0.0, 1.0, perm)
            r = 1.0 / (1.0 + s)
            ah[plane, here] = (1.0 - s) * r
            bh[plane, here] = 0.5 * r
            se = s / eff
            r = 1.0 / (1.0 + se)
            ae[plane, here] = (1.0 - se) * r
            b = 0.5 * r / eff
            be[plane, here] = b
            bm[plane, here] = jnp.where(mat == 2.0, 0.5 * b, 0.0)

    for g in range(GROUPS):
        with scope("ghosts"):
            for step in (-1, 1):
                columns(g, step).wait()
        with scope("build"):
            build(g)
        if g == 0:
            for step in (-1, 1):
                layers(step).start()
            loop(OWN, OWN + 4, coefficients)
        if g == 1:
            loop(OWN, OWN + 4, lambda x: edges_e(e, x)())

    def trace_e(step):
        return pltpu.make_async_remote_copy(
            src_ref=send_e.at[step], dst_ref=recv_e.at[step],
            send_sem=se_sem.at[step], recv_sem=re_sem.at[step],
            device_id=towards("gx", -1), device_id_type=MESH,
        )

    def trace_h(step):
        return pltpu.make_async_remote_copy(
            src_ref=send_h.at[step], dst_ref=recv_h.at[step],
            send_sem=sh_sem.at[step], recv_sem=rh_sem.at[step],
            device_id=towards("gx", 1), device_id_type=MESH,
        )

    def give(ref, plane, out, step):
        for c in range(2):
            for t in range(TILES):
                out[step, c, pl.ds(8 * t, 8)] = ref[plane, at(1 + c, t)]

    def take(ref, plane, trace, step):
        for c in range(2):
            for t in range(TILES):
                ref[CROSS, at(1 + c, t)] = ref[plane, at(1 + c, t)] + trace[step, c, pl.ds(8 * t, 8)]

    def block(b, carry):
        size = 4 - b // 2
        start = 4 * b - b // 3

        def free_h(x, base):
            nxt = base + x + 1 + (x // 3) * (ZERO_E - base - 4)
            h_pass(e, h, ah, bh, base + x, nxt, FREE + x, OWN + x)

        def free_e(x, base):
            e_pass(e, h, j, p, q, ae, be, bm, base + x, FREE + x, FREE + x - 1, FREE + x, OWN + x)

        def give_e(plane, step):
            give(e, plane, send_e, step)
            trace_e(step).start()

        def give_h(step):
            give(h, FREE + 3, send_h, step)
            trace_h(step).start()

        def free(i):
            base = OWN + ((i + 3) // 4) * (FREE - OWN)
            last = (i + 2) // size
            give_e(base, start + i)
            store = edges_e(e, base + 2)
            free_h(3, base)
            store()
            give_h(start + i)

            def more_h(x):
                store = edges_h(h, FREE + x - 1 + 4 * (1 - (x + 2) // 3))
                free_h(x, base)
                store()

            loop(0, 3, more_h)
            store = edges_h(h, FREE + 2)
            free_e(3, base)
            store()

            def more_e(x):
                store = edges_e(e, FREE + x - 1 + 4 * (1 - (x + 2) // 3))
                free_e(x, base)
                store()

            loop(0, 3 - 2 * last, more_e)

        with scope("free"):
            loop(0, size - 1, free)
            give_e(FREE, start + size - 1)
            free_h(3, FREE)
            give_h(start + size - 1)

        with scope("clear"):
            clear((0, 1, 6, 7), (e, h, j, p, q))

        def ghost_coefficients(i):
            for step in (-1, 1):
                layers(step).wait()
            loop(0, 2, coefficients)
            loop(6, 8, coefficients)

        with scope("ghostcoef"):
            loop(0, 1 - (b + 3) // 4, ghost_coefficients)

        def true(i):
            step = start + i
            first = 1 - (i + 3) // 4
            final = (i + 1) // size
            edge = first + final
            deep = ((i + 3) // 4) * (1 - (i + 2) // size)
            ghost = 1 - final

            def true_h(x):
                h_pass(e, h, ah, bh, x, x + 1 + 2 * (x // 5) * (1 - x // 6), x, x)

            def true_e(x, prv):
                e_pass(e, h, j, p, q, ae, be, bm, x, x, prv, x, x)

            def more_h(x):
                store = edges_h(h, x - 1)
                true_h(x)
                store()

            store = edges_e(e, 2)
            true_h(edge)
            store()
            loop(edge + 1, 5, more_h)
            with scope("wait_e"):
                trace_e(step).wait_recv()
            take(e, 6, recv_e, step)
            loop(5, 7 - edge, more_h)

            top = 6 + ghost + deep
            store = edges_h(h, 6 - edge)
            true_e(3, 2)
            store()

            def more_e(x):
                store = edges_e(e, x - 1)
                true_e(x, x - 1)
                store()

            loop(4, top, more_e)
            with scope("wait_h"):
                trace_h(step).wait_recv()
            take(h, 1, recv_h, step)

            low = 2 - ghost - deep

            def bottom(x):
                begun = (x - low + 3) // 4
                store = edges_e(e, begun * (x - 1) + (1 - begun) * (top - 1))
                true_e(x, x - 1 + 10 * (1 - (x + 1) // 2) + 7 * (x // 2))
                store()

            loop(low, 3, bottom)

        with scope("true"):
            loop(0, size, true)
            edges_e(e, 2)()
        return carry

    lax.fori_loop(0, BLOCKS, block, 0)

    def finish(step):
        trace_e(step).wait_send()
        trace_h(step).wait_send()

    with scope("finish"):
        loop(0, STEPS, finish)

    results = [(e, c) for c in range(3)] + [(h, c) for c in range(3)]
    with scope("results"):
        for g in range(2):
            group = results[4 * g : 4 * g + 4]

            def gather(t):
                tiles = [ref[OWN + x, pl.ds(pl.multiple_of(COMP * c + TILE * (t + 1), 8), 8)] for ref, c in group for x in range(4)]
                tiles = tiles + tiles[: 16 - len(tiles)]
                whole = jnp.transpose(jnp.concatenate(tiles, 0))
                for zb in range(8):
                    turned[g, zb, pl.ds(t, 16, stride=10)] = whole[16 * zb : 16 * zb + 16]

            loop(0, TILES, gather)

            def spread(zb):
                whole = jnp.transpose(turned[g, zb, pl.ds(16, 128)])
                for s in range(len(group)):
                    for x in range(4):
                        stage[4 * g + s, zb, pl.ds(x, 8, stride=4)] = whole[32 * s + 8 * x : 32 * s + 8 * x + 8]

            loop(0, 8, spread)
            if g == 0:
                pltpu.make_async_copy(stage.at[pl.ds(0, 3)], e_out, in_sem.at[0]).start()
        pltpu.make_async_copy(stage.at[pl.ds(3, 3)], h_out, in_sem.at[1]).start()
        pltpu.make_async_copy(stage.at[pl.ds(0, 3)], e_out, in_sem.at[0]).wait()
        pltpu.make_async_copy(stage.at[pl.ds(3, 3)], h_out, in_sem.at[1]).wait()


def shards(
    e_field, h_field, drude_current, lorentz_polar, lorentz_rate, permittivity, material, absorber
):
    fields = [f.reshape(3, 8, 32, 128) for f in (e_field, h_field, drude_current, lorentz_polar, lorentz_rate)]
    cells = [c.reshape(8, 32, 128) for c in (permittivity, material, absorber)]
    wide = pltpu.VMEM((PLANES, 3 * COMP, 128), F32)
    narrow = pltpu.VMEM((PLANES, 3 * ROWS, 128), F32)
    cell = pltpu.VMEM((8, ROWS, 128), F32)
    trace = pltpu.VMEM((STEPS, 2, ROWS, 128), F32)
    out = jax.ShapeDtypeStruct((3, 8, 32, 128), F32)
    e, h = pl.pallas_call(
        kernel,
        out_shape=(out, out),
        in_specs=[pl.BlockSpec(memory_space=pl.ANY)] * 8,
        out_specs=(pl.BlockSpec(memory_space=pl.ANY),) * 2,
        scratch_shapes=[
            pltpu.VMEM((18, 8, 32, 128), F32),
            pltpu.VMEM((2, 8, 32, 128), jnp.int32),
            pltpu.VMEM((GROUPS, 8, 160, 128), F32),
            pltpu.VMEM((8, 3, ROWS, 128), F32),
            wide, wide, narrow, narrow, narrow,
            cell, cell, cell, cell, cell,
            trace, trace, trace, trace,
            pltpu.SemaphoreType.DMA((8,)),
            pltpu.SemaphoreType.DMA((2, 2 * GROUPS)),
            pltpu.SemaphoreType.DMA((2, 2)),
            pltpu.SemaphoreType.DMA((STEPS,)),
            pltpu.SemaphoreType.DMA((STEPS,)),
            pltpu.SemaphoreType.DMA((STEPS,)),
            pltpu.SemaphoreType.DMA((STEPS,)),
        ],
        compiler_params=pltpu.CompilerParams(
            collective_id=0, has_side_effects=True, vmem_limit_bytes=48 * 1024 * 1024
        ),
    )(*(pltpu.with_memory_space_constraint(a, pltpu.HBM) for a in (*fields, *cells)))
    return e.reshape(3, 64, 4, 128), h.reshape(3, 64, 4, 128)


def solution(mesh):
    field, cell = P(None, None, "gx", "gy"), P(None, "gx", "gy")
    return jax.shard_map(
        shards, mesh=mesh, in_specs=(field,) * 5 + (cell,) * 3, out_specs=(field, field), check_vma=False
    )
```

```python
import contextlib

import jax
import jax.numpy as jnp
from jax import lax
from jax.experimental import pallas as pl
from jax.experimental.pallas import tpu as pltpu
from jax.sharding import PartitionSpec as P

STEPS = 14
BLOCKS = 4
MESH = pl.DeviceIdType.MESH
NAMED = False
F32 = jnp.float32

TILES = 10
TILE = 16
COMP = 12 * TILE
ROWS = 80
OWN = 2
CROSS = 8
ZERO_H = 9
FREE = 10
ZERO_E = 14
PLANES = 15

C_J = 0.975 / 1.025
C_E = 2.0 * (1.125 / 1.025)

SLOTS = ["perm", "mat", "abs", "e0", "e1", "e2", "h0", "h1", "h2", "j0", "j1", "j2", "p0", "p1", "p2", "q0", "q1", "q2"]
GROUPS = 5
GHOST = STEPS


def scope(name):
    return jax.named_scope(name) if NAMED else contextlib.nullcontext()


def towards(axis, step):
    count = lax.axis_size(axis)
    return {axis: lax.rem(lax.axis_index(axis) + step + count, count)}


def lanes(rows=8):
    return lax.broadcasted_iota(jnp.int32, (rows, 128), 1)


def loop(low, high, body):
    lax.fori_loop(low, high, lambda i, carry: (body(i), carry)[1], 0)


def loop_twice(count, body):
    loop(0, count // 2, lambda i: (body(2 * i), body(2 * i + 1)))


def at(c, t, shift=0):
    return pl.ds(COMP * c + TILE * (t + 1) + shift, 8)


def packed(c, t):
    return pl.ds(ROWS * c + 8 * t, 8)


class Tiles:
    def __init__(self, ref, plane):
        self.ref, self.plane, self.held = ref, plane, {}

    def __call__(self, c, t):
        if (c, t) not in self.held:
            self.held[c, t] = self.ref[self.plane, at(c, t)]
        return self.held[c, t]


@contextlib.contextmanager
def later(*stores):
    yield
    for store in stores:
        store()


def pipelined(load, work):
    loaded = load(0)
    for t in range(TILES):
        later = load(t + 1) if t + 1 < TILES else None
        work(t, loaded)
        loaded = later


def h_pass(e, h, ah, bh, src, nxt, dst, cell):
    tile = Tiles(e, src)

    def load(t):
        here = pl.ds(8 * t, 8)
        return (
            [tile(c, t) for c in range(3)],
            tile(0, t + 1), tile(2, t + 1),
            e[src, at(0, t, 1)], e[src, at(1, t, 1)],
            e[nxt, at(1, t)], e[nxt, at(2, t)],
            [h[src, at(c, t)] for c in range(3)],
            ah[cell, here], bh[cell, here],
        )

    def work(t, loaded):
        (ex, ey, ez), ex_y, ez_y, ex_z, ey_z, ey_x, ez_x, (hx, hy, hz), a, b = loaded
        h[dst, at(0, t)] = a * hx - b * ((ez_y - ez) - (ey_z - ey))
        h[dst, at(1, t)] = a * hy - b * ((ex_z - ex) - (ez_x - ez))
        h[dst, at(2, t)] = a * hz - b * ((ey_x - ey) - (ex_y - ex))

    pipelined(load, work)


def e_pass(e, h, j, p, q, ae, be, bm, src, mag, prv, dst, cell):
    tile = Tiles(h, mag)

    def load(t):
        here = pl.ds(8 * t, 8)
        media = [(e[src, at(c, t)], j[src, packed(c, t)], p[src, packed(c, t)], q[src, packed(c, t)]) for c in range(3)]
        return (
            media,
            [tile(c, t) for c in range(3)],
            tile(0, t - 1), tile(2, t - 1),
            h[mag, at(0, t, -1)], h[mag, at(1, t, -1)],
            h[prv, at(1, t)], h[prv, at(2, t)],
            ae[cell, here], be[cell, here], bm[cell, here],
        )

    def work(t, loaded):
        media, (hx, hy, hz), hx_y, hz_y, hx_z, hy_z, hy_x, hz_x, a, b, m = loaded
        curl = (
            (hz - hz_y) - (hy - hy_z),
            (hx - hx_z) - (hz - hz_x),
            (hy - hy_x) - (hx - hx_y),
        )
        for c in range(3):
            ec, jc, pc, qc = media[c]
            jc = C_J * jc + C_E * ec
            qc = 0.9 * qc + (ec - pc)
            pc = pc + 0.25 * qc
            j[dst, packed(c, t)] = jc
            q[dst, packed(c, t)] = qc
            p[dst, packed(c, t)] = pc
            e[dst, at(c, t)] = a * ec + (b * curl[c] - m * (jc + qc))

    pipelined(load, work)


def edges_e(e, plane):
    tiles = [e[plane, at(c, 0)] for c in (0, 2)]
    first = e[plane, pl.ds(0, 24, stride=TILE)]
    tiles = [pltpu.roll(tile, 127, 1) for tile in tiles]
    first = jnp.where(lanes(24) < 112, pltpu.roll(first, 112, 1), 0.0)

    def store():
        e[plane, at(0, TILES)], e[plane, at(2, TILES)] = tiles
        e[plane, pl.ds(8, 24, stride=TILE)] = first

    return store


def edges_h(h, plane):
    tiles = [h[plane, at(c, TILES - 1)] for c in (0, 2)]
    last = h[plane, pl.ds(TILE + 7, 24, stride=TILE)]
    tiles = [pltpu.roll(tile, 1, 1) for tile in tiles]
    last = jnp.where(lanes(24) < 16, 0.0, pltpu.roll(last, 16, 1))

    def store():
        h[plane, at(0, -1)], h[plane, at(2, -1)] = tiles
        h[plane, pl.ds(TILE - 1, 24, stride=TILE)] = last

    return store


def kernel(
    e_in, h_in, j_in, p_in, q_in, perm_in, mat_in, abs_in, e_out, h_out,
    stage, ints, turned, raw, e, h, j, p, q, ah, bh, ae, be, bm,
    send_e, send_h, recv_e, recv_h, in_sem, y_sem, x_sem, se_sem, re_sem, sh_sem, rh_sem,
):
    def blank(zb):
        for g in range(GROUPS):
            for edge in (0, 152):
                turned[g, zb, pl.ds(edge, 8)] = jnp.zeros((8, 128), F32)

    loop(0, 8, blank)

    barrier = pltpu.get_barrier_semaphore()
    for axis in ("gx", "gy"):
        for step in (-1, 1):
            pl.semaphore_signal(barrier, inc=1, device_id=towards(axis, step), device_id_type=MESH)

    fields = (e_in, h_in, j_in, p_in, q_in)
    loads = {
        "perm": pltpu.make_async_copy(perm_in, stage.at[0], in_sem.at[5]),
        "mat": pltpu.make_async_copy(mat_in, ints.at[0], in_sem.at[6]),
        "abs": pltpu.make_async_copy(abs_in, ints.at[1], in_sem.at[7]),
    }
    for i, f in enumerate(fields):
        loads["ehjpq"[i]] = pltpu.make_async_copy(f, stage.at[pl.ds(3 + 3 * i, 3)], in_sem.at[i])
    for load in loads.values():
        load.start()

    def clear(planes, refs):
        for ref in refs:
            size = ref.shape[1] // 6

            def body(i):
                for plane in planes:
                    for k in range(size // 8):
                        ref[plane, pl.ds(pl.multiple_of(size * i + 8 * k, 8), 8)] = jnp.zeros((8, 128), F32)

            loop(0, 6, body)

    clear((ZERO_E,), (e,))
    clear((ZERO_H,), (h,))

    def turn(g):
        slots = range(4 * g, min(4 * g + 4, len(SLOTS)))

        def body(zb):
            rows = []
            for block in (zb,) if g < 4 else (zb, zb + 4):
                for slot in slots:
                    for x in range(4):
                        here = pl.ds(x, 8, stride=4)
                        if slot in (1, 2):
                            rows.append(ints[slot - 1, block, here].astype(F32))
                        else:
                            rows.append(stage[slot, block, here])
            turned[g, zb, pl.ds(16, 128)] = jnp.transpose(jnp.concatenate(rows, 0))

        loop_twice(8 if g < 4 else 4, body)

    def columns(g, step):
        source, target = (pl.ds(16, GHOST), pl.ds(144, GHOST)) if step < 0 else (pl.ds(144 - GHOST, GHOST), pl.ds(16 - GHOST, GHOST))
        k = 2 * g + (step + 1) // 2
        blocks = pl.ds(0, 8 if g < 4 else 4)
        return pltpu.make_async_remote_copy(
            src_ref=turned.at[g, blocks, source], dst_ref=turned.at[g, blocks, target],
            send_sem=y_sem.at[0, k], recv_sem=y_sem.at[1, k],
            device_id=towards("gy", step), device_id_type=MESH,
        )

    waited = set()
    for g in range(GROUPS):
        with scope("turn"):
            for name in SLOTS[4 * g : 4 * g + 4]:
                name = name if name in loads else name[0]
                if name not in waited:
                    waited.add(name)
                    loads[name].wait()
            turn(g)
        if g == 0:
            with scope("barrier"):
                pl.semaphore_wait(barrier, 4)
        for step in (-1, 1):
            columns(g, step).start()

    state = {"e": e, "h": h, "j": j, "p": p, "q": q}

    def build(g):
        def body(t):
            rows = jnp.concatenate([turned[g, zb, pl.ds(t, 16, stride=10)] for zb in range(8 if g < 4 else 4)], 0)
            if g == 4:
                rows = jnp.concatenate([rows, pltpu.roll(rows, 64, 1)], 0)
            whole = jnp.transpose(rows)
            for s, name in enumerate(SLOTS[4 * g : 4 * g + 4]):
                for x in range(4):
                    part = whole[32 * s + 8 * x : 32 * s + 8 * x + 8]
                    if 4 * g + s < 3:
                        raw[OWN + x, 4 * g + s, pl.ds(pl.multiple_of(8 * t, 8), 8)] = part
                        continue
                    c = int(name[1])
                    if name[0] in "eh":
                        row = COMP * c + TILE * (t + 1)
                    else:
                        row = ROWS * c + 8 * t
                    if name[0] in "jq":
                        part = part * 2.0
                    state[name[0]][OWN + x, pl.ds(pl.multiple_of(row, 8), 8)] = part

        loop_twice(TILES, body)

    def layers(step):
        source, target = (OWN, OWN + 4) if step < 0 else (OWN + 2, OWN - 2)
        k = (step + 1) // 2
        return pltpu.make_async_remote_copy(
            src_ref=raw.at[pl.ds(source, 2)], dst_ref=raw.at[pl.ds(target, 2)],
            send_sem=x_sem.at[0, k], recv_sem=x_sem.at[1, k],
            device_id=towards("gx", step), device_id_type=MESH,
        )

    def coefficients(plane):
        for t in range(TILES):
            here = pl.ds(8 * t, 8)
            perm, mat, absorb = (raw[plane, i, here] for i in range(3))
            s = 0.1 * absorb
            eff = jnp.where(mat == 0.0, 1.0, perm)
            r = 1.0 / (1.0 + s)
            ah[plane, here] = (1.0 - s) * r
            bh[plane, here] = 0.5 * r
            se = s / eff
            r = 1.0 / (1.0 + se)
            ae[plane, here] = (1.0 - se) * r
            b = 0.5 * r / eff
            be[plane, here] = b
            bm[plane, here] = jnp.where(mat == 2.0, 0.5 * b, 0.0)

    for g in range(GROUPS):
        with scope("ghosts"):
            for step in (-1, 1):
                columns(g, step).wait()
        with scope("build"):
            build(g)
        if g == 0:
            for step in (-1, 1):
                layers(step).start()
            loop(OWN, OWN + 4, coefficients)
        if g == 1:
            loop(OWN, OWN + 4, lambda x: edges_e(e, x)())

    def trace_e(step):
        return pltpu.make_async_remote_copy(
            src_ref=send_e.at[step], dst_ref=recv_e.at[step],
            send_sem=se_sem.at[step], recv_sem=re_sem.at[step],
            device_id=towards("gx", -1), device_id_type=MESH,
        )

    def trace_h(step):
        return pltpu.make_async_remote_copy(
            src_ref=send_h.at[step], dst_ref=recv_h.at[step],
            send_sem=sh_sem.at[step], recv_sem=rh_sem.at[step],
            device_id=towards("gx", 1), device_id_type=MESH,
        )

    def give(ref, plane, out, step):
        for c in range(2):
            for t in range(TILES):
                out[step, c, pl.ds(8 * t, 8)] = ref[plane, at(1 + c, t)]

    def take(ref, plane, trace, step):
        for c in range(2):
            for t in range(TILES):
                ref[CROSS, at(1 + c, t)] = ref[plane, at(1 + c, t)] + trace[step, c, pl.ds(8 * t, 8)]

    def block(b, carry):
        size = 4 - b // 2
        start = 4 * b - b // 3

        def free_h(x, src, dst):
            nxt = src + x + 1 + (x // 3) * (ZERO_E - src - 4)
            h_pass(e, h, ah, bh, src + x, nxt, dst + x, OWN + x)

        def free_e(x, src, dst):
            prv = dst + x - 1 + (1 - (x + 2) // 3) * (ZERO_H - dst + 1)
            e_pass(e, h, j, p, q, ae, be, bm, src + x, dst + x, prv, dst + x, OWN + x)

        def give_e(plane, step):
            give(e, plane, send_e, step)
            trace_e(step).start()

        def give_h(plane, step):
            give(h, plane, send_h, step)
            trace_h(step).start()

        def free(i):
            src = OWN + (i // 2) * (FREE - OWN)
            dst = OWN + ((i + 3) // 4) * (FREE - OWN)
            last = (i + 2) // size
            give_e(src, start + i)
            with later(*(edges_e(e, src + x) for x in range(3))):
                free_h(3, src, dst)
            give_h(dst + 3, start + i)
            with later(edges_h(h, dst + 3)):
                free_h(0, src, dst)
                free_h(1, src, dst)
                free_h(2, src, dst)
            with later(edges_h(h, dst)):
                free_e(3, src, dst)
            with later(edges_e(e, dst + 3), edges_h(h, dst + 1), edges_h(h, dst + 2)):
                free_e(0, src, dst)

            def inner(_):
                free_e(1, src, dst)
                free_e(2, src, dst)

            loop(last, 1, inner)

        with scope("free"):
            loop(0, size - 1, free)
            give_e(FREE, start + size - 1)
            free_h(3, FREE, FREE)
            give_h(FREE + 3, start + size - 1)

        with scope("clear"):
            clear((0, 1, 6, 7), (e, h))
            clear((1, 6), (j, p, q))

        def ghost_coefficients(i):
            for step in (-1, 1):
                layers(step).wait()
            loop(0, 2, coefficients)
            loop(6, 8, coefficients)

        with scope("ghostcoef"):
            loop(0, 1 - (b + 3) // 4, ghost_coefficients)

        def from_own(cell, mag, plane):
            for t in range(TILES):
                b = be[cell, pl.ds(8 * t, 8)]
                hy, hz = h[mag, at(1, t)], h[mag, at(2, t)]
                curl = (hz - h[mag, at(2, t - 1)]) - (hy - h[mag, at(1, t, -1)])
                e[plane, at(0, t)] = e[plane, at(0, t)] + b * curl
                e[plane, at(1, t)] = e[plane, at(1, t)] - b * hz
                e[plane, at(2, t)] = e[plane, at(2, t)] + b * hy

        def from_below(mag, plane):
            for t in range(TILES):
                b = be[plane, pl.ds(8 * t, 8)]
                e[plane, at(1, t)] = b * h[mag, at(2, t)]
                e[plane, at(2, t)] = -b * h[mag, at(1, t)]

        def answer(trace, cell, delta, plane):
            for t in range(TILES):
                here = pl.ds(8 * t, 8)
                b = bh[cell, here]
                hy, hz = b * trace[start, 1, here], b * trace[start, 0, here]
                h[delta, at(1, t)] = hy
                h[delta, at(2, t)] = -hz
                if delta != plane:
                    h[plane, at(1, t)] = h[plane, at(1, t)] + hy
                    h[plane, at(2, t)] = h[plane, at(2, t)] - hz
            edges_h(h, delta)()
            from_own(cell, delta, plane)

        with scope("first"):
            answer(send_e, 1, 1, 1)
            with scope("wait_e"):
                trace_e(start).wait_recv()
            answer(recv_e, 5, FREE + 3, 5)
            from_below(5, 6)
            with scope("wait_h"):
                trace_h(start).wait_recv()
            for t in range(TILES):
                here = pl.ds(8 * t, 8)
                b = be[2, here]
                e[2, at(1, t)] = e[2, at(1, t)] + b * (h[1, at(2, t)] + recv_h[start, 1, here])
                e[2, at(2, t)] = e[2, at(2, t)] - b * (h[1, at(1, t)] + recv_h[start, 0, here])

        def true(i):
            step = start + i
            final = (i + 1) // size
            deep = 1 - (i + 2) // size

            def true_h(x, nxt):
                h_pass(e, h, ah, bh, x, nxt, x, x)

            def true_e(x, prv):
                e_pass(e, h, j, p, q, ae, be, bm, x, x, prv, x, x)

            with later(*(edges_e(e, x) for x in (0, 1, 2, 5, 6))):
                true_h(3, 4)
                true_h(4, 5)
            with later(edges_h(h, 3), edges_h(h, 4)):
                true_h(1, 2)
                true_h(2, 3)
            loop(final, 1, lambda _: true_h(0, 1))
            with scope("wait_e"):
                trace_e(step).wait_recv()
            take(e, 6, recv_e, step)
            true_h(5, CROSS)
            loop(final, 1, lambda _: true_h(6, 7))

            with later(*(edges_h(h, x) for x in (1, 2, 5, 6))):
                true_e(3, 2)
                true_e(4, 3)
            with later(edges_e(e, 3), edges_e(e, 4), edges_h(h, 0)):
                true_e(5, 4)
            loop(final, 1, lambda _: true_e(6, 5))
            loop(1 - deep, 1, lambda _: from_below(6, 7))
            with scope("wait_h"):
                trace_h(step).wait_recv()
            take(h, 1, recv_h, step)
            with later(edges_e(e, 5)):
                true_e(2, CROSS)
            loop(final, 1, lambda _: true_e(1, 0))
            loop(1 - deep, 1, lambda _: from_own(0, 0, 0))

        with scope("true"):
            loop(1, size, true)
        return carry

    lax.fori_loop(0, BLOCKS, block, 0)

    def finish(step):
        trace_e(step).wait_send()
        trace_h(step).wait_send()

    with scope("finish"):
        loop(0, STEPS, finish)

    results = [(e, c) for c in range(3)] + [(h, c) for c in range(3)]
    with scope("results"):
        for g in range(2):
            group = results[4 * g : 4 * g + 4]

            def gather(t):
                tiles = [ref[OWN + x, pl.ds(pl.multiple_of(COMP * c + TILE * (t + 1), 8), 8)] for ref, c in group for x in range(4)]
                tiles = tiles + tiles[: 16 - len(tiles)]
                whole = jnp.transpose(jnp.concatenate(tiles, 0))
                for zb in range(8):
                    turned[g, zb, pl.ds(t, 16, stride=10)] = whole[16 * zb : 16 * zb + 16]

            loop_twice(TILES, gather)

            def spread(zb):
                whole = jnp.transpose(turned[g, zb, pl.ds(16, 128)])
                for s in range(len(group)):
                    for x in range(4):
                        stage[4 * g + s, zb, pl.ds(x, 8, stride=4)] = whole[32 * s + 8 * x : 32 * s + 8 * x + 8]

            loop_twice(8, spread)
            if g == 0:
                pltpu.make_async_copy(stage.at[pl.ds(0, 3)], e_out, in_sem.at[0]).start()
        pltpu.make_async_copy(stage.at[pl.ds(3, 3)], h_out, in_sem.at[1]).start()
        pltpu.make_async_copy(stage.at[pl.ds(0, 3)], e_out, in_sem.at[0]).wait()
        pltpu.make_async_copy(stage.at[pl.ds(3, 3)], h_out, in_sem.at[1]).wait()


def shards(
    e_field, h_field, drude_current, lorentz_polar, lorentz_rate, permittivity, material, absorber
):
    fields = [f.reshape(3, 8, 32, 128) for f in (e_field, h_field, drude_current, lorentz_polar, lorentz_rate)]
    cells = [c.reshape(8, 32, 128) for c in (permittivity, material, absorber)]
    wide = pltpu.VMEM((PLANES, 3 * COMP, 128), F32)
    narrow = pltpu.VMEM((PLANES, 3 * ROWS, 128), F32)
    cell = pltpu.VMEM((8, ROWS, 128), F32)
    trace = pltpu.VMEM((STEPS, 2, ROWS, 128), F32)
    out = jax.ShapeDtypeStruct((3, 8, 32, 128), F32)
    e, h = pl.pallas_call(
        kernel,
        out_shape=(out, out),
        in_specs=[pl.BlockSpec(memory_space=pl.ANY)] * 8,
        out_specs=(pl.BlockSpec(memory_space=pl.ANY),) * 2,
        scratch_shapes=[
            pltpu.VMEM((18, 8, 32, 128), F32),
            pltpu.VMEM((2, 8, 32, 128), jnp.int32),
            pltpu.VMEM((GROUPS, 8, 160, 128), F32),
            pltpu.VMEM((8, 3, ROWS, 128), F32),
            wide, wide, narrow, narrow, narrow,
            cell, cell, cell, cell, cell,
            trace, trace, trace, trace,
            pltpu.SemaphoreType.DMA((8,)),
            pltpu.SemaphoreType.DMA((2, 2 * GROUPS)),
            pltpu.SemaphoreType.DMA((2, 2)),
            pltpu.SemaphoreType.DMA((STEPS,)),
            pltpu.SemaphoreType.DMA((STEPS,)),
            pltpu.SemaphoreType.DMA((STEPS,)),
            pltpu.SemaphoreType.DMA((STEPS,)),
        ],
        compiler_params=pltpu.CompilerParams(
            collective_id=0, has_side_effects=True, vmem_limit_bytes=48 * 1024 * 1024
        ),
    )(*(pltpu.with_memory_space_constraint(a, pltpu.HBM) for a in (*fields, *cells)))
    return e.reshape(3, 64, 4, 128), h.reshape(3, 64, 4, 128)


def solution(mesh):
    field, cell = P(None, None, "gx", "gy"), P(None, "gx", "gy")
    return jax.shard_map(
        shards, mesh=mesh, in_specs=(field,) * 5 + (cell,) * 3, out_specs=(field, field), check_vma=False
    )
```

```python
import contextlib

import jax
import jax.numpy as jnp
from jax import lax
from jax.experimental import pallas as pl
from jax.experimental.pallas import tpu as pltpu
from jax.sharding import PartitionSpec as P

STEPS = 14
BLOCKS = 4
MESH = pl.DeviceIdType.MESH
NAMED = False
F32 = jnp.float32

TILES = 10
TILE = 16
COMP = 12 * TILE
ROWS = 80
OWN = 2
CROSS = 8
ZERO_H = 9
FREE = 10
ZERO_E = 14
PLANES = 15

C_J = 0.975 / 1.025
C_E = 2.0 * (1.125 / 1.025)

SLOTS = ["perm", "mat", "abs", "e0", "e1", "e2", "h0", "h1", "h2", "j0", "j1", "j2", "p0", "p1", "p2", "q0", "q1", "q2"]
GROUPS = 5
GHOST = STEPS


def scope(name):
    return jax.named_scope(name) if NAMED else contextlib.nullcontext()


def towards(axis, step):
    count = lax.axis_size(axis)
    return {axis: lax.rem(lax.axis_index(axis) + step + count, count)}


def lanes(rows=8):
    return lax.broadcasted_iota(jnp.int32, (rows, 128), 1)


def loop(low, high, body):
    lax.fori_loop(low, high, lambda i, carry: (body(i), carry)[1], 0)


def loop_twice(count, body):
    loop(0, count // 2, lambda i: (body(2 * i), body(2 * i + 1)))


def at(c, t, shift=0):
    return pl.ds(COMP * c + TILE * (t + 1) + shift, 8)


def packed(c, t):
    return pl.ds(ROWS * c + 8 * t, 8)


class Tiles:
    def __init__(self, ref, plane):
        self.ref, self.plane, self.held = ref, plane, {}

    def __call__(self, c, t):
        if (c, t) not in self.held:
            self.held[c, t] = self.ref[self.plane, at(c, t)]
        return self.held[c, t]


@contextlib.contextmanager
def later(*stores):
    yield
    for store in stores:
        store()


def pipelined(load, work):
    loaded = load(0)
    for t in range(TILES):
        later = load(t + 1) if t + 1 < TILES else None
        work(t, loaded)
        loaded = later


def h_pass(e, h, ah, bh, src, nxt, dst, cell):
    tile = Tiles(e, src)

    def load(t):
        here = pl.ds(8 * t, 8)
        return (
            [tile(c, t) for c in range(3)],
            tile(0, t + 1), tile(2, t + 1),
            e[src, at(0, t, 1)], e[src, at(1, t, 1)],
            e[nxt, at(1, t)], e[nxt, at(2, t)],
            [h[src, at(c, t)] for c in range(3)],
            ah[cell, here], bh[cell, here],
        )

    def work(t, loaded):
        (ex, ey, ez), ex_y, ez_y, ex_z, ey_z, ey_x, ez_x, (hx, hy, hz), a, b = loaded
        h[dst, at(0, t)] = a * hx - b * ((ez_y - ez) - (ey_z - ey))
        h[dst, at(1, t)] = a * hy - b * ((ex_z - ex) - (ez_x - ez))
        h[dst, at(2, t)] = a * hz - b * ((ey_x - ey) - (ex_y - ex))

    pipelined(load, work)


def e_pass(e, h, j, p, q, ae, be, bm, src, mag, prv, dst, cell):
    tile = Tiles(h, mag)

    def load(t):
        here = pl.ds(8 * t, 8)
        media = [(e[src, at(c, t)], j[src, packed(c, t)], p[src, packed(c, t)], q[src, packed(c, t)]) for c in range(3)]
        return (
            media,
            [tile(c, t) for c in range(3)],
            tile(0, t - 1), tile(2, t - 1),
            h[mag, at(0, t, -1)], h[mag, at(1, t, -1)],
            h[prv, at(1, t)], h[prv, at(2, t)],
            ae[cell, here], be[cell, here], bm[cell, here],
        )

    def work(t, loaded):
        media, (hx, hy, hz), hx_y, hz_y, hx_z, hy_z, hy_x, hz_x, a, b, m = loaded
        curl = (
            (hz - hz_y) - (hy - hy_z),
            (hx - hx_z) - (hz - hz_x),
            (hy - hy_x) - (hx - hx_y),
        )
        for c in range(3):
            ec, jc, pc, qc = media[c]
            jc = C_J * jc + C_E * ec
            qc = 0.9 * qc + (ec - pc)
            pc = pc + 0.25 * qc
            j[dst, packed(c, t)] = jc
            q[dst, packed(c, t)] = qc
            p[dst, packed(c, t)] = pc
            e[dst, at(c, t)] = a * ec + (b * curl[c] - m * (jc + qc))

    pipelined(load, work)


def edges_e(e, plane):
    tiles = [e[plane, at(c, 0)] for c in (0, 2)]
    first = e[plane, pl.ds(0, 24, stride=TILE)]
    tiles = [pltpu.roll(tile, 127, 1) for tile in tiles]
    first = jnp.where(lanes(24) < 112, pltpu.roll(first, 112, 1), 0.0)

    def store():
        e[plane, at(0, TILES)], e[plane, at(2, TILES)] = tiles
        e[plane, pl.ds(8, 24, stride=TILE)] = first

    return store


def edges_h(h, plane):
    tiles = [h[plane, at(c, TILES - 1)] for c in (0, 2)]
    last = h[plane, pl.ds(TILE + 7, 24, stride=TILE)]
    tiles = [pltpu.roll(tile, 1, 1) for tile in tiles]
    last = jnp.where(lanes(24) < 16, 0.0, pltpu.roll(last, 16, 1))

    def store():
        h[plane, at(0, -1)], h[plane, at(2, -1)] = tiles
        h[plane, pl.ds(TILE - 1, 24, stride=TILE)] = last

    return store


def kernel(
    e_in, h_in, j_in, p_in, q_in, perm_in, mat_in, abs_in, e_out, h_out,
    stage, ints, turned, raw, e, h, j, p, q, ah, bh, ae, be, bm,
    send_e, send_h, recv_e, recv_h, in_sem, y_sem, x_sem, s_sem, re_sem, rh_sem,
):
    def blank(zb):
        for g in range(GROUPS):
            for edge in (0, 152):
                turned[g, zb, pl.ds(edge, 8)] = jnp.zeros((8, 128), F32)

    loop(0, 8, blank)

    barrier = pltpu.get_barrier_semaphore()
    for axis in ("gx", "gy"):
        for step in (-1, 1):
            pl.semaphore_signal(barrier, inc=1, device_id=towards(axis, step), device_id_type=MESH)

    fields = (e_in, h_in, j_in, p_in, q_in)
    pltpu.make_async_copy(perm_in, stage.at[0], in_sem.at[0]).start()
    pltpu.make_async_copy(mat_in, ints.at[0], in_sem.at[0]).start()
    pltpu.make_async_copy(abs_in, ints.at[1], in_sem.at[0]).start()
    for i, f in enumerate(fields):
        pltpu.make_async_copy(f, stage.at[pl.ds(3 + 3 * i, 3)], in_sem.at[i]).start()

    def arrive(ref, sem):
        pltpu.make_async_copy(ref, ref, sem).wait()

    def clear(planes, refs):
        for ref in refs:
            size = ref.shape[1] // 6

            def body(i):
                for plane in planes:
                    for k in range(size // 8):
                        ref[plane, pl.ds(pl.multiple_of(size * i + 8 * k, 8), 8)] = jnp.zeros((8, 128), F32)

            loop(0, 6, body)

    clear((ZERO_E,), (e,))
    clear((ZERO_H,), (h,))

    def turn(g):
        slots = range(4 * g, min(4 * g + 4, len(SLOTS)))

        def body(zb):
            rows = []
            for block in (zb,) if g < 4 else (zb, zb + 4):
                for slot in slots:
                    for x in range(4):
                        here = pl.ds(x, 8, stride=4)
                        if slot in (1, 2):
                            rows.append(ints[slot - 1, block, here].astype(F32))
                        else:
                            rows.append(stage[slot, block, here])
            turned[g, zb, pl.ds(16, 128)] = jnp.transpose(jnp.concatenate(rows, 0))

        loop_twice(8 if g < 4 else 4, body)

    def columns(g, step):
        source, target = (pl.ds(16, GHOST), pl.ds(144, GHOST)) if step < 0 else (pl.ds(144 - GHOST, GHOST), pl.ds(16 - GHOST, GHOST))
        blocks = pl.ds(0, 8 if g < 4 else 4)
        return pltpu.make_async_remote_copy(
            src_ref=turned.at[g, blocks, source], dst_ref=turned.at[g, blocks, target],
            send_sem=y_sem.at[GROUPS], recv_sem=y_sem.at[g],
            device_id=towards("gy", step), device_id_type=MESH,
        )

    for g in range(GROUPS):
        with scope("turn"):
            if g < 4:
                arrive(stage.at[pl.ds(0, 6)] if g == 0 else stage.at[pl.ds(3 + 3 * g, 3)], in_sem.at[g])
            if g == 3:
                arrive(stage.at[pl.ds(15, 3)], in_sem.at[4])
            turn(g)
        if g == 0:
            with scope("barrier"):
                pl.semaphore_wait(barrier, 4)
        for step in (-1, 1):
            columns(g, step).start()

    state = {"e": e, "h": h, "j": j, "p": p, "q": q}

    def build(g):
        def body(t):
            rows = jnp.concatenate([turned[g, zb, pl.ds(t, 16, stride=10)] for zb in range(8 if g < 4 else 4)], 0)
            if g == 4:
                rows = jnp.concatenate([rows, pltpu.roll(rows, 64, 1)], 0)
            whole = jnp.transpose(rows)
            for s, name in enumerate(SLOTS[4 * g : 4 * g + 4]):
                for x in range(4):
                    part = whole[32 * s + 8 * x : 32 * s + 8 * x + 8]
                    if 4 * g + s < 3:
                        raw[OWN + x, 4 * g + s, pl.ds(pl.multiple_of(8 * t, 8), 8)] = part
                        continue
                    c = int(name[1])
                    if name[0] in "eh":
                        row = COMP * c + TILE * (t + 1)
                    else:
                        row = ROWS * c + 8 * t
                    if name[0] in "jq":
                        part = part * 2.0
                    state[name[0]][OWN + x, pl.ds(pl.multiple_of(row, 8), 8)] = part

        loop_twice(TILES, body)

    def layers(step):
        source, target = (OWN, OWN + 4) if step < 0 else (OWN + 2, OWN - 2)
        return pltpu.make_async_remote_copy(
            src_ref=raw.at[pl.ds(source, 2)], dst_ref=raw.at[pl.ds(target, 2)],
            send_sem=x_sem.at[0], recv_sem=x_sem.at[1],
            device_id=towards("gx", step), device_id_type=MESH,
        )

    def coefficients(plane):
        for t in range(TILES):
            here = pl.ds(8 * t, 8)
            perm, mat, absorb = (raw[plane, i, here] for i in range(3))
            s = 0.1 * absorb
            eff = jnp.where(mat == 0.0, 1.0, perm)
            r = 1.0 / (1.0 + s)
            ah[plane, here] = (1.0 - s) * r
            bh[plane, here] = 0.5 * r
            se = s / eff
            r = 1.0 / (1.0 + se)
            ae[plane, here] = (1.0 - se) * r
            b = 0.5 * r / eff
            be[plane, here] = b
            bm[plane, here] = jnp.where(mat == 2.0, 0.5 * b, 0.0)

    def trace_e(step, mark):
        return pltpu.make_async_remote_copy(
            src_ref=send_e.at[step], dst_ref=recv_e.at[step],
            send_sem=s_sem.at[0], recv_sem=re_sem.at[mark],
            device_id=towards("gx", -1), device_id_type=MESH,
        )

    def trace_h(step, mark):
        return pltpu.make_async_remote_copy(
            src_ref=send_h.at[step], dst_ref=recv_h.at[step],
            send_sem=s_sem.at[1], recv_sem=rh_sem.at[mark],
            device_id=towards("gx", 1), device_id_type=MESH,
        )

    def give(ref, plane, out, step):
        for c in range(2):
            for t in range(TILES):
                out[step, c, pl.ds(8 * t, 8)] = ref[plane, at(1 + c, t)]

    def take(ref, plane, trace, step):
        for c in range(2):
            for t in range(TILES):
                ref[CROSS, at(1 + c, t)] = ref[plane, at(1 + c, t)] + trace[step, c, pl.ds(8 * t, 8)]

    def free_h(x, src, dst):
        nxt = src + x + 1 + (x // 3) * (ZERO_E - src - 4)
        h_pass(e, h, ah, bh, src + x, nxt, dst + x, OWN + x)

    def free_e(x, src, dst):
        prv = dst + x - 1 + (1 - (x + 2) // 3) * (ZERO_H - dst + 1)
        e_pass(e, h, j, p, q, ae, be, bm, src + x, dst + x, prv, dst + x, OWN + x)

    def give_e(plane, step, mark):
        give(e, plane, send_e, step)
        trace_e(step, mark).start()

    def give_h(plane, step, mark):
        give(h, plane, send_h, step)
        trace_h(step, mark).start()

    def h_part(src, dst, step, mark):
        give_e(src, step, mark)
        with later(*(edges_e(e, src + x) for x in range(3))):
            free_h(3, src, dst)
        give_h(dst + 3, step, mark)
        with later(edges_h(h, dst + 3)):
            free_h(0, src, dst)
            free_h(1, src, dst)
            free_h(2, src, dst)

    for g in range(GROUPS):
        with scope("ghosts"):
            arrive(turned.at[g, pl.ds(0, 8 if g < 4 else 4), pl.ds(0, 2 * GHOST)], y_sem.at[g])
        with scope("build"):
            build(g)
        if g == 0:
            for step in (-1, 1):
                layers(step).start()
            loop(OWN, OWN + 4, coefficients)
        if g == 1:
            loop(OWN, OWN + 4, lambda x: edges_e(e, x)())
        if g == 2:
            h_part(OWN, OWN, 0, 0)

    def block(b, carry):
        size = 4 - b // 2
        start = 4 * b - b // 3
        marks = 4 * lax.rem(b, 2) - start

        def free(i):
            src = OWN + (i // 2) * (FREE - OWN)
            dst = OWN + ((i + 3) // 4) * (FREE - OWN)
            last = (i + 2) // size
            loop(1 - (i + 3) // 4, 1, lambda _: h_part(src, dst, start + i, marks + start + i))
            with later(edges_h(h, dst)):
                free_e(3, src, dst)
            with later(edges_e(e, dst + 3), edges_h(h, dst + 1), edges_h(h, dst + 2)):
                free_e(0, src, dst)

            def inner(_):
                free_e(1, src, dst)
                free_e(2, src, dst)

            loop(last, 1, inner)

        with scope("free"):
            loop(0, size - 1, free)
            final = start + size - 1
            give_e(FREE, final, marks + final)
            free_h(3, FREE, FREE)
            give_h(FREE + 3, final, marks + final)

        with scope("clear"):
            clear((0, 1, 6, 7), (e, h))
            clear((1, 6), (j, p, q))

        def ghost_coefficients(i):
            arrive(raw.at[pl.ds(0, 4)], x_sem.at[1])
            loop(0, 2, coefficients)
            loop(6, 8, coefficients)

        with scope("ghostcoef"):
            loop(0, 1 - (b + 3) // 4, ghost_coefficients)

        def from_own(cell, mag, plane):
            for t in range(TILES):
                b = be[cell, pl.ds(8 * t, 8)]
                hy, hz = h[mag, at(1, t)], h[mag, at(2, t)]
                curl = (hz - h[mag, at(2, t - 1)]) - (hy - h[mag, at(1, t, -1)])
                e[plane, at(0, t)] = e[plane, at(0, t)] + b * curl
                e[plane, at(1, t)] = e[plane, at(1, t)] - b * hz
                e[plane, at(2, t)] = e[plane, at(2, t)] + b * hy

        def from_below(mag, plane):
            for t in range(TILES):
                b = be[plane, pl.ds(8 * t, 8)]
                e[plane, at(1, t)] = b * h[mag, at(2, t)]
                e[plane, at(2, t)] = -b * h[mag, at(1, t)]

        def answer(trace, cell, delta, plane):
            for t in range(TILES):
                here = pl.ds(8 * t, 8)
                b = bh[cell, here]
                hy, hz = b * trace[start, 1, here], b * trace[start, 0, here]
                h[delta, at(1, t)] = hy
                h[delta, at(2, t)] = -hz
                if delta != plane:
                    h[plane, at(1, t)] = h[plane, at(1, t)] + hy
                    h[plane, at(2, t)] = h[plane, at(2, t)] - hz
            edges_h(h, delta)()
            from_own(cell, delta, plane)

        with scope("first"):
            answer(send_e, 1, 1, 1)
            with scope("wait_e"):
                trace_e(start, marks + start).wait_recv()
            answer(recv_e, 5, FREE + 3, 5)
            from_below(5, 6)
            with scope("wait_h"):
                trace_h(start, marks + start).wait_recv()
            for t in range(TILES):
                here = pl.ds(8 * t, 8)
                own = be[2, here]
                e[2, at(1, t)] = e[2, at(1, t)] + own * (h[1, at(2, t)] + recv_h[start, 1, here])
                e[2, at(2, t)] = e[2, at(2, t)] - own * (h[1, at(1, t)] + recv_h[start, 0, here])

        def true(i):
            step = start + i
            final = (i + 1) // size
            deep = 1 - (i + 2) // size

            def true_h(x, nxt):
                h_pass(e, h, ah, bh, x, nxt, x, x)

            def true_e(x, prv):
                e_pass(e, h, j, p, q, ae, be, bm, x, x, prv, x, x)

            with later(*(edges_e(e, x) for x in (0, 1, 2, 5, 6))):
                true_h(3, 4)
                true_h(4, 5)
            with later(edges_h(h, 3), edges_h(h, 4)):
                true_h(1, 2)
                true_h(2, 3)
            loop(final, 1, lambda _: true_h(0, 1))
            with scope("wait_e"):
                trace_e(step, marks + step).wait_recv()
            take(e, 6, recv_e, step)
            true_h(5, CROSS)
            loop(final, 1, lambda _: true_h(6, 7))

            with later(*(edges_h(h, x) for x in (1, 2, 5, 6))):
                true_e(3, 2)
                true_e(4, 3)
            with later(edges_e(e, 3), edges_e(e, 4), edges_h(h, 0)):
                true_e(5, 4)
            loop(final, 1, lambda _: true_e(6, 5))
            loop(1 - deep, 1, lambda _: from_below(6, 7))
            with scope("wait_h"):
                trace_h(step, marks + step).wait_recv()
            take(h, 1, recv_h, step)
            with later(edges_e(e, 5)):
                true_e(2, CROSS)
            loop(final, 1, lambda _: true_e(1, 0))
            loop(1 - deep, 1, lambda _: from_own(0, 0, 0))

        with scope("true"):
            loop(1, size, true)

        def onward(_):
            h_part(OWN, OWN, start + size, 4 * lax.rem(b + 1, 2))

        loop(b // 3, 1, onward)
        return carry

    lax.fori_loop(0, BLOCKS, block, 0)

    with scope("finish"):
        arrive(send_e, s_sem.at[0])
        arrive(send_h, s_sem.at[1])
        arrive(raw.at[pl.ds(0, 4)], x_sem.at[0])
        arrive(turned.at[0, :, pl.ds(0, 9 * GHOST)], y_sem.at[GROUPS])

    results = [(e, c) for c in range(3)] + [(h, c) for c in range(3)]
    outs = [(e_out, c) for c in range(3)] + [(h_out, c) for c in range(3)]
    with scope("results"):
        for g in range(2):
            group = results[4 * g : 4 * g + 4]

            def gather(t):
                tiles = [ref[OWN + x, pl.ds(pl.multiple_of(COMP * c + TILE * (t + 1), 8), 8)] for ref, c in group for x in range(4)]
                tiles = tiles + tiles[: 16 - len(tiles)]
                whole = jnp.transpose(jnp.concatenate(tiles, 0))
                for zb in range(8):
                    turned[g, zb, pl.ds(t, 16, stride=10)] = whole[16 * zb : 16 * zb + 16]

            loop_twice(TILES, gather)

            def spread(zb):
                whole = jnp.transpose(turned[g, zb, pl.ds(16, 128)])
                for s in range(len(group)):
                    for x in range(4):
                        out, c = outs[4 * g + s]
                        out[c, zb, pl.ds(x, 8, stride=4)] = whole[32 * s + 8 * x : 32 * s + 8 * x + 8]

            loop_twice(8, spread)

def hand_out(e, h, e_out, h_out, sem):
    copies = [
        pltpu.make_async_copy(ref.at[c], out.at[c], sem.at[3 * i + c])
        for i, (ref, out) in enumerate(((e, e_out), (h, h_out)))
        for c in range(3)
    ]
    for copy in copies:
        copy.start()
    for copy in copies:
        copy.wait()


def shards(
    e_field, h_field, drude_current, lorentz_polar, lorentz_rate, permittivity, material, absorber
):
    fields = [f.reshape(3, 8, 32, 128) for f in (e_field, h_field, drude_current, lorentz_polar, lorentz_rate)]
    cells = [c.reshape(8, 32, 128) for c in (permittivity, material, absorber)]
    wide = pltpu.VMEM((PLANES, 3 * COMP, 128), F32)
    narrow = pltpu.VMEM((PLANES, 3 * ROWS, 128), F32)
    cell = pltpu.VMEM((8, ROWS, 128), F32)
    trace = pltpu.VMEM((STEPS, 2, ROWS, 128), F32)
    e, h = pl.pallas_call(
        kernel,
        out_shape=(pltpu.VMEM((3, 8, 32, 128), F32),) * 2,
        in_specs=[pl.BlockSpec(memory_space=pl.ANY)] * 8,
        out_specs=(pl.BlockSpec(memory_space=pltpu.VMEM),) * 2,
        scratch_shapes=[
            pltpu.VMEM((18, 8, 32, 128), F32),
            pltpu.VMEM((2, 8, 32, 128), jnp.int32),
            pltpu.VMEM((GROUPS, 8, 160, 128), F32),
            pltpu.VMEM((8, 3, ROWS, 128), F32),
            wide, wide, narrow, narrow, narrow,
            cell, cell, cell, cell, cell,
            trace, trace, trace, trace,
            pltpu.SemaphoreType.DMA((5,)),
            pltpu.SemaphoreType.DMA((GROUPS + 1,)),
            pltpu.SemaphoreType.DMA((2,)),
            pltpu.SemaphoreType.DMA((2,)),
            pltpu.SemaphoreType.DMA((8,)),
            pltpu.SemaphoreType.DMA((8,)),
        ],
        compiler_params=pltpu.CompilerParams(
            collective_id=0, has_side_effects=True, vmem_limit_bytes=48 * 1024 * 1024
        ),
    )(*(pltpu.with_memory_space_constraint(a, pltpu.HBM) for a in (*fields, *cells)))
    e, h = pl.pallas_call(
        hand_out,
        out_shape=(jax.ShapeDtypeStruct((3, 8, 32, 128), F32),) * 2,
        in_specs=[pl.BlockSpec(memory_space=pltpu.VMEM)] * 2,
        out_specs=(pl.BlockSpec(memory_space=pltpu.HBM),) * 2,
        scratch_shapes=[pltpu.SemaphoreType.DMA((6,))],
    )(*(pltpu.with_memory_space_constraint(a, pltpu.VMEM) for a in (e, h)))
    return e.reshape(3, 64, 4, 128), h.reshape(3, 64, 4, 128)


def solution(mesh):
    field, cell = P(None, None, "gx", "gy"), P(None, "gx", "gy")
    return jax.shard_map(
        shards, mesh=mesh, in_specs=(field,) * 5 + (cell,) * 3, out_specs=(field, field), check_vma=False
    )
```

```python
import contextlib

import jax
import jax.numpy as jnp
from jax import lax
from jax.experimental import pallas as pl
from jax.experimental.pallas import tpu as pltpu
from jax.sharding import PartitionSpec as P

STEPS = 14
BLOCKS = 4
MESH = pl.DeviceIdType.MESH
NAMED = False
F32 = jnp.float32

TILES = 10
TILE = 16
COMP = 12 * TILE
ROWS = 80
OWN = 2
CROSS = 8
ZERO_H = 9
FREE = 10
ZERO_E = 14
PLANES = 15

C_J = 0.975 / 1.025
C_E = 2.0 * (1.125 / 1.025)

SLOTS = ["perm", "mat", "abs", "e0", "e1", "e2", "h0", "h1", "h2", "j0", "j1", "j2", "p0", "p1", "p2", "q0", "q1", "q2"]
GROUPS = 5
GHOST = STEPS


def scope(name):
    return jax.named_scope(name) if NAMED else contextlib.nullcontext()


def towards(axis, step):
    count = lax.axis_size(axis)
    return {axis: lax.rem(lax.axis_index(axis) + step + count, count)}


def lanes(rows=8):
    return lax.broadcasted_iota(jnp.int32, (rows, 128), 1)


def loop(low, high, body):
    lax.fori_loop(low, high, lambda i, carry: (body(i), carry)[1], 0)


def loop_by(size, count, body):
    loop(0, count // size, lambda i: [body(size * i + k) for k in range(size)])


def at(c, t, shift=0):
    return pl.ds(COMP * c + TILE * (t + 1) + shift, 8)


def packed(c, t):
    return pl.ds(ROWS * c + 8 * t, 8)


class Tiles:
    def __init__(self, ref, plane):
        self.ref, self.plane, self.held = ref, plane, {}

    def __call__(self, c, t):
        if (c, t) not in self.held:
            self.held[c, t] = self.ref[self.plane, at(c, t)]
        return self.held[c, t]


@contextlib.contextmanager
def later(*stores):
    yield
    for store in stores:
        store()


def pipelined(load, work):
    loaded = load(0)
    for t in range(TILES):
        later = load(t + 1) if t + 1 < TILES else None
        work(t, loaded)
        loaded = later


def h_pass(e, h, ah, bh, src, nxt, dst, cell):
    tile = Tiles(e, src)

    def load(t):
        here = pl.ds(8 * t, 8)
        return (
            [tile(c, t) for c in range(3)],
            tile(0, t + 1), tile(2, t + 1),
            e[src, at(0, t, 1)], e[src, at(1, t, 1)],
            e[nxt, at(1, t)], e[nxt, at(2, t)],
            [h[src, at(c, t)] for c in range(3)],
            ah[cell, here], bh[cell, here],
        )

    def work(t, loaded):
        (ex, ey, ez), ex_y, ez_y, ex_z, ey_z, ey_x, ez_x, (hx, hy, hz), a, b = loaded
        h[dst, at(0, t)] = a * hx - b * ((ez_y - ez) - (ey_z - ey))
        h[dst, at(1, t)] = a * hy - b * ((ex_z - ex) - (ez_x - ez))
        h[dst, at(2, t)] = a * hz - b * ((ey_x - ey) - (ex_y - ex))

    pipelined(load, work)


def e_pass(e, h, j, p, q, ae, be, bm, src, mag, prv, dst, cell):
    tile = Tiles(h, mag)

    def load(t):
        here = pl.ds(8 * t, 8)
        media = [(e[src, at(c, t)], j[src, packed(c, t)], p[src, packed(c, t)], q[src, packed(c, t)]) for c in range(3)]
        return (
            media,
            [tile(c, t) for c in range(3)],
            tile(0, t - 1), tile(2, t - 1),
            h[mag, at(0, t, -1)], h[mag, at(1, t, -1)],
            h[prv, at(1, t)], h[prv, at(2, t)],
            ae[cell, here], be[cell, here], bm[cell, here],
        )

    def work(t, loaded):
        media, (hx, hy, hz), hx_y, hz_y, hx_z, hy_z, hy_x, hz_x, a, b, m = loaded
        curl = (
            (hz - hz_y) - (hy - hy_z),
            (hx - hx_z) - (hz - hz_x),
            (hy - hy_x) - (hx - hx_y),
        )
        for c in range(3):
            ec, jc, pc, qc = media[c]
            jc = C_J * jc + C_E * ec
            qc = 0.9 * qc + (ec - pc)
            pc = pc + 0.25 * qc
            j[dst, packed(c, t)] = jc
            q[dst, packed(c, t)] = qc
            p[dst, packed(c, t)] = pc
            e[dst, at(c, t)] = a * ec + (b * curl[c] - m * (jc + qc))

    pipelined(load, work)


def edges_e(e, plane):
    tiles = [e[plane, at(c, 0)] for c in (0, 2)]
    first = e[plane, pl.ds(0, 24, stride=TILE)]
    tiles = [pltpu.roll(tile, 127, 1) for tile in tiles]
    first = jnp.where(lanes(24) < 112, pltpu.roll(first, 112, 1), 0.0)

    def store():
        e[plane, at(0, TILES)], e[plane, at(2, TILES)] = tiles
        e[plane, pl.ds(8, 24, stride=TILE)] = first

    return store


def edges_h(h, plane):
    tiles = [h[plane, at(c, TILES - 1)] for c in (0, 2)]
    last = h[plane, pl.ds(TILE + 7, 24, stride=TILE)]
    tiles = [pltpu.roll(tile, 1, 1) for tile in tiles]
    last = jnp.where(lanes(24) < 16, 0.0, pltpu.roll(last, 16, 1))

    def store():
        h[plane, at(0, -1)], h[plane, at(2, -1)] = tiles
        h[plane, pl.ds(TILE - 1, 24, stride=TILE)] = last

    return store


def kernel(
    e_in, h_in, j_in, p_in, q_in, perm_in, mat_in, abs_in, e_out, h_out,
    stage, ints, turned, raw, e, h, j, p, q, ah, bh, ae, be, bm,
    send_e, send_h, recv_e, recv_h, in_sem, y_sem, x_sem, s_sem, re_sem, rh_sem,
):
    def blank(zb):
        for g in range(GROUPS):
            for edge in (0, 152):
                turned[g, zb, pl.ds(edge, 8)] = jnp.zeros((8, 128), F32)

    loop(0, 8, blank)

    barrier = pltpu.get_barrier_semaphore()
    for axis in ("gx", "gy"):
        for step in (-1, 1):
            pl.semaphore_signal(barrier, inc=1, device_id=towards(axis, step), device_id_type=MESH)

    fields = (e_in, h_in, j_in, p_in, q_in)
    pltpu.make_async_copy(perm_in, stage.at[0], in_sem.at[0]).start()
    pltpu.make_async_copy(mat_in, ints.at[0], in_sem.at[0]).start()
    pltpu.make_async_copy(abs_in, ints.at[1], in_sem.at[0]).start()
    for i, f in enumerate(fields):
        pltpu.make_async_copy(f, stage.at[pl.ds(3 + 3 * i, 3)], in_sem.at[i]).start()

    def arrive(ref, sem):
        pltpu.make_async_copy(ref, ref, sem).wait()

    def clear(planes, refs):
        for ref in refs:
            size = ref.shape[1] // 6

            def body(i):
                for plane in planes:
                    for k in range(size // 8):
                        ref[plane, pl.ds(pl.multiple_of(size * i + 8 * k, 8), 8)] = jnp.zeros((8, 128), F32)

            loop(0, 6, body)

    clear((ZERO_E,), (e,))
    clear((ZERO_H,), (h,))

    def turn(g):
        slots = range(4 * g, min(4 * g + 4, len(SLOTS)))

        def body(zb):
            rows = []
            for block in (zb,) if g < 4 else (zb, zb + 4):
                for slot in slots:
                    for x in range(4):
                        here = pl.ds(x, 8, stride=4)
                        if slot in (1, 2):
                            rows.append(ints[slot - 1, block, here].astype(F32))
                        else:
                            rows.append(stage[slot, block, here])
            turned[g, zb, pl.ds(16, 128)] = jnp.transpose(jnp.concatenate(rows, 0))

        loop_by(2, 8 if g < 4 else 4, body)

    def columns(g, step):
        source, target = (pl.ds(16, GHOST), pl.ds(144, GHOST)) if step < 0 else (pl.ds(144 - GHOST, GHOST), pl.ds(16 - GHOST, GHOST))
        blocks = pl.ds(0, 8 if g < 4 else 4)
        return pltpu.make_async_remote_copy(
            src_ref=turned.at[g, blocks, source], dst_ref=turned.at[g, blocks, target],
            send_sem=y_sem.at[GROUPS], recv_sem=y_sem.at[g],
            device_id=towards("gy", step), device_id_type=MESH,
        )

    for g in range(GROUPS):
        with scope("turn"):
            if g < 4:
                arrive(stage.at[pl.ds(0, 6)] if g == 0 else stage.at[pl.ds(3 + 3 * g, 3)], in_sem.at[g])
            if g == 3:
                arrive(stage.at[pl.ds(15, 3)], in_sem.at[4])
            turn(g)
        if g == 0:
            with scope("barrier"):
                pl.semaphore_wait(barrier, 4)
        for step in (-1, 1):
            columns(g, step).start()

    state = {"e": e, "h": h, "j": j, "p": p, "q": q}

    def build(g):
        def body(t):
            rows = jnp.concatenate([turned[g, zb, pl.ds(t, 16, stride=10)] for zb in range(8 if g < 4 else 4)], 0)
            if g == 4:
                rows = jnp.concatenate([rows, pltpu.roll(rows, 64, 1)], 0)
                rows = rows[:, :64]
            whole = jnp.transpose(rows)
            for s, name in enumerate(SLOTS[4 * g : 4 * g + 4]):
                for x in range(4):
                    part = whole[32 * s + 8 * x : 32 * s + 8 * x + 8]
                    if 4 * g + s < 3:
                        raw[OWN + x, 4 * g + s, pl.ds(pl.multiple_of(8 * t, 8), 8)] = part
                        continue
                    c = int(name[1])
                    if name[0] in "eh":
                        row = COMP * c + TILE * (t + 1)
                    else:
                        row = ROWS * c + 8 * t
                    if name[0] in "jq":
                        part = part * 2.0
                    state[name[0]][OWN + x, pl.ds(pl.multiple_of(row, 8), 8)] = part

        loop_by(2 if g < 4 else 5, TILES, body)

    def layer(source, target, step, k):
        return pltpu.make_async_remote_copy(
            src_ref=source, dst_ref=target, send_sem=x_sem.at[3], recv_sem=x_sem.at[k],
            device_id=towards("gx", step), device_id_type=MESH,
        )

    def coefficients(plane, h_alone=False):
        for t in range(TILES):
            here = pl.ds(8 * t, 8)
            s = 0.1 * raw[plane, 2, here]
            r = 1.0 / (1.0 + s)
            ah[plane, here] = (1.0 - s) * r
            bh[plane, here] = 0.5 * r
            if h_alone:
                continue
            perm, mat = raw[plane, 0, here], raw[plane, 1, here]
            eff = jnp.where(mat == 0.0, 1.0, perm)
            se = s / eff
            r = 1.0 / (1.0 + se)
            ae[plane, here] = (1.0 - se) * r
            b = 0.5 * r / eff
            be[plane, here] = b
            bm[plane, here] = jnp.where(mat == 2.0, 0.5 * b, 0.0)

    def trace_e(step, mark):
        return pltpu.make_async_remote_copy(
            src_ref=send_e.at[step], dst_ref=recv_e.at[step],
            send_sem=s_sem.at[0], recv_sem=re_sem.at[mark],
            device_id=towards("gx", -1), device_id_type=MESH,
        )

    def trace_h(step, mark):
        return pltpu.make_async_remote_copy(
            src_ref=send_h.at[step], dst_ref=recv_h.at[step],
            send_sem=s_sem.at[1], recv_sem=rh_sem.at[mark],
            device_id=towards("gx", 1), device_id_type=MESH,
        )

    def give(ref, plane, out, step):
        for c in range(2):
            for t in range(TILES):
                out[step, c, pl.ds(8 * t, 8)] = ref[plane, at(1 + c, t)]

    def take(ref, plane, trace, step):
        for c in range(2):
            for t in range(TILES):
                ref[CROSS, at(1 + c, t)] = ref[plane, at(1 + c, t)] + trace[step, c, pl.ds(8 * t, 8)]

    def free_h(x, src, dst):
        nxt = src + x + 1 + (x // 3) * (ZERO_E - src - 4)
        h_pass(e, h, ah, bh, src + x, nxt, dst + x, OWN + x)

    def free_e(x, src, dst):
        prv = dst + x - 1 + (1 - (x + 2) // 3) * (ZERO_H - dst + 1)
        e_pass(e, h, j, p, q, ae, be, bm, src + x, dst + x, prv, dst + x, OWN + x)

    def give_e(plane, step, mark):
        give(e, plane, send_e, step)
        trace_e(step, mark).start()

    def give_h(plane, step, mark):
        give(h, plane, send_h, step)
        trace_h(step, mark).start()

    def h_part(src, dst, step, mark):
        give_e(src, step, mark)
        with later(*(edges_e(e, src + x) for x in range(3))):
            free_h(3, src, dst)
        give_h(dst + 3, step, mark)
        with later(edges_h(h, dst + 3)):
            free_h(0, src, dst)
            free_h(1, src, dst)
            free_h(2, src, dst)

    for g in range(GROUPS):
        with scope("ghosts"):
            arrive(turned.at[g, pl.ds(0, 8 if g < 4 else 4), pl.ds(0, 2 * GHOST)], y_sem.at[g])
        with scope("build"):
            build(g)
        if g == 0:
            layer(raw.at[OWN], raw.at[OWN + 4], -1, 0).start()
            layer(raw.at[OWN + 3], raw.at[OWN - 1], 1, 0).start()
            layer(raw.at[OWN + 2, 2], raw.at[OWN - 2, 2], 1, 1).start()
            loop(OWN, OWN + 4, coefficients)
        if g == 1:
            loop(OWN, OWN + 4, lambda x: edges_e(e, x)())
        if g == 2:
            h_part(OWN, OWN, 0, 0)
            layer(be.at[OWN + 1], be.at[OWN + 5], -1, 2).start()
            layer(be.at[OWN + 2], be.at[OWN - 2], 1, 2).start()

    def block(b, carry):
        size = 3 + b // 2
        start = 3 * b + b // 3
        marks = 4 * lax.rem(b, 2) - start

        def free(i):
            src = OWN + (i // 2) * (FREE - OWN)
            dst = OWN + ((i + 3) // 4) * (FREE - OWN)
            last = (i + 2) // size
            loop(1 - (i + 3) // 4, 1, lambda _: h_part(src, dst, start + i, marks + start + i))
            with later(edges_h(h, dst)):
                free_e(3, src, dst)
            with later(edges_e(e, dst + 3), edges_h(h, dst + 1), edges_h(h, dst + 2)):
                free_e(0, src, dst)

            def inner(_):
                free_e(1, src, dst)
                free_e(2, src, dst)

            loop(last, 1, inner)

        with scope("free"):
            loop(0, size - 1, free)
            final = start + size - 1
            give_e(FREE, final, marks + final)
            free_h(3, FREE, FREE)
            give_h(FREE + 3, final, marks + final)

        with scope("clear"):
            clear((0, 1, 6, 7), (e, h))
            clear((1, 6), (j, p, q))

        def ghost_coefficients(_):
            arrive(raw.at[pl.ds(0, 2)], x_sem.at[0])
            coefficients(1)
            coefficients(6)
            arrive(raw.at[0, 2], x_sem.at[1])
            coefficients(0, h_alone=True)

        with scope("ghostcoef"):
            loop((b + 3) // 4, 1, ghost_coefficients)
            loop(1 - (b // 2) * (1 - b // 3), 1, lambda _: arrive(be.at[pl.ds(0, 2)], x_sem.at[2]))

        def from_own(cell, mag, plane):
            for t in range(TILES):
                b = be[cell, pl.ds(8 * t, 8)]
                hy, hz = h[mag, at(1, t)], h[mag, at(2, t)]
                curl = (hz - h[mag, at(2, t - 1)]) - (hy - h[mag, at(1, t, -1)])
                e[plane, at(0, t)] = e[plane, at(0, t)] + b * curl
                e[plane, at(1, t)] = e[plane, at(1, t)] - b * hz
                e[plane, at(2, t)] = e[plane, at(2, t)] + b * hy

        def from_below(mag, plane):
            for t in range(TILES):
                b = be[plane, pl.ds(8 * t, 8)]
                e[plane, at(1, t)] = b * h[mag, at(2, t)]
                e[plane, at(2, t)] = -b * h[mag, at(1, t)]

        def answer(trace, cell, delta, plane):
            for t in range(TILES):
                here = pl.ds(8 * t, 8)
                b = bh[cell, here]
                hy, hz = b * trace[start, 1, here], b * trace[start, 0, here]
                h[delta, at(1, t)] = hy
                h[delta, at(2, t)] = -hz
                if delta != plane:
                    h[plane, at(1, t)] = h[plane, at(1, t)] + hy
                    h[plane, at(2, t)] = h[plane, at(2, t)] - hz
            edges_h(h, delta)()
            from_own(cell, delta, plane)

        with scope("first"):
            answer(send_e, 1, 1, 1)
            with scope("wait_e"):
                trace_e(start, marks + start).wait_recv()
            answer(recv_e, 5, FREE + 3, 5)
            from_below(5, 6)
            with scope("wait_h"):
                trace_h(start, marks + start).wait_recv()
            for t in range(TILES):
                here = pl.ds(8 * t, 8)
                own = be[2, here]
                e[2, at(1, t)] = e[2, at(1, t)] + own * (h[1, at(2, t)] + recv_h[start, 1, here])
                e[2, at(2, t)] = e[2, at(2, t)] - own * (h[1, at(1, t)] + recv_h[start, 0, here])

        def true(i):
            step = start + i
            final = (i + 1) // size
            deep = 1 - (i + 2) // size

            def true_h(x, nxt):
                h_pass(e, h, ah, bh, x, nxt, x, x)

            def true_e(x, prv):
                e_pass(e, h, j, p, q, ae, be, bm, x, x, prv, x, x)

            with later(*(edges_e(e, x) for x in (0, 1, 2, 5, 6))):
                true_h(3, 4)
                true_h(4, 5)
            with later(edges_h(h, 3), edges_h(h, 4)):
                true_h(1, 2)
                true_h(2, 3)
            loop(final, 1, lambda _: true_h(0, 1))
            with later(edges_h(h, 0), edges_h(h, 1), edges_h(h, 2)):
                true_e(3, 2)
                true_e(4, 3)
            loop(final, 1, lambda _: true_e(1, 0))
            with scope("wait_e"):
                trace_e(step, marks + step).wait_recv()
            take(e, 6, recv_e, step)
            with later(edges_e(e, 3), edges_e(e, 4)):
                true_h(5, CROSS)
            loop(final, 1, lambda _: true_h(6, 7))
            for store in (edges_h(h, 5), edges_h(h, 6)):
                store()
            true_e(5, 4)
            loop(final, 1, lambda _: true_e(6, 5))
            loop(1 - deep, 1, lambda _: from_below(6, 7))
            with scope("wait_h"):
                trace_h(step, marks + step).wait_recv()
            take(h, 1, recv_h, step)
            with later(edges_e(e, 5)):
                true_e(2, CROSS)
            loop(1 - deep, 1, lambda _: from_own(0, 0, 0))

        with scope("true"):
            loop(1, size, true)

        def onward(_):
            h_part(OWN, OWN, start + size, 4 * lax.rem(b + 1, 2))

        loop(b // 3, 1, onward)
        return carry

    lax.fori_loop(0, BLOCKS, block, 0)

    with scope("finish"):
        arrive(send_e, s_sem.at[0])
        arrive(send_h, s_sem.at[1])
        arrive(raw.at[pl.ds(0, 3)], x_sem.at[3])
        arrive(turned.at[0, :, pl.ds(0, 9 * GHOST)], y_sem.at[GROUPS])

    results = [(e, c) for c in range(3)] + [(h, c) for c in range(3)]
    outs = [(e_out, c) for c in range(3)] + [(h_out, c) for c in range(3)]
    with scope("results"):
        def gather(t):
            for g in range(2):
                group = results[4 * g : 4 * g + 4]
                tiles = [ref[OWN + x, pl.ds(pl.multiple_of(COMP * c + TILE * (t + 1), 8), 8)] for ref, c in group for x in range(4)]
                tiles = jnp.concatenate(tiles, 0)
                if g == 1:
                    tiles = jnp.concatenate([tiles, pltpu.roll(tiles, 64, 1)], 0)[:, :64]
                whole = jnp.transpose(tiles)
                for zb in range(8 if g == 0 else 4):
                    turned[g, zb, pl.ds(t, 16, stride=10)] = whole[16 * zb : 16 * zb + 16]

        loop_by(2, TILES, gather)

        def spread(g, zb):
            whole = jnp.transpose(turned[g, zb, pl.ds(16, 128)])
            group = outs[4 * g : 4 * g + 4]
            row = 0
            for block in (zb,) if g == 0 else (zb, zb + 4):
                for out, c in group:
                    for x in range(4):
                        out[c, block, pl.ds(x, 8, stride=4)] = whole[row : row + 8]
                        row += 8

        loop(0, 4, lambda zb: (spread(0, 2 * zb), spread(0, 2 * zb + 1), spread(1, zb)))


def hand_out(e, h, e_out, h_out, sem):
    copies = [
        pltpu.make_async_copy(ref.at[c], out.at[c], sem.at[3 * i + c])
        for i, (ref, out) in enumerate(((e, e_out), (h, h_out)))
        for c in range(3)
    ]
    for copy in copies:
        copy.start()
    for copy in copies:
        copy.wait()


def shards(
    e_field, h_field, drude_current, lorentz_polar, lorentz_rate, permittivity, material, absorber
):
    fields = [f.reshape(3, 8, 32, 128) for f in (e_field, h_field, drude_current, lorentz_polar, lorentz_rate)]
    cells = [c.reshape(8, 32, 128) for c in (permittivity, material, absorber)]
    wide = pltpu.VMEM((PLANES, 3 * COMP, 128), F32)
    narrow = pltpu.VMEM((PLANES, 3 * ROWS, 128), F32)
    cell = pltpu.VMEM((8, ROWS, 128), F32)
    trace = pltpu.VMEM((STEPS, 2, ROWS, 128), F32)
    e, h = pl.pallas_call(
        kernel,
        out_shape=(pltpu.VMEM((3, 8, 32, 128), F32),) * 2,
        in_specs=[pl.BlockSpec(memory_space=pl.ANY)] * 8,
        out_specs=(pl.BlockSpec(memory_space=pltpu.VMEM),) * 2,
        scratch_shapes=[
            pltpu.VMEM((18, 8, 32, 128), F32),
            pltpu.VMEM((2, 8, 32, 128), jnp.int32),
            pltpu.VMEM((GROUPS, 8, 160, 128), F32),
            pltpu.VMEM((8, 3, ROWS, 128), F32),
            wide, wide, narrow, narrow, narrow,
            cell, cell, cell, cell, cell,
            trace, trace, trace, trace,
            pltpu.SemaphoreType.DMA((5,)),
            pltpu.SemaphoreType.DMA((GROUPS + 1,)),
            pltpu.SemaphoreType.DMA((4,)),
            pltpu.SemaphoreType.DMA((2,)),
            pltpu.SemaphoreType.DMA((8,)),
            pltpu.SemaphoreType.DMA((8,)),
        ],
        compiler_params=pltpu.CompilerParams(
            collective_id=0, has_side_effects=True, vmem_limit_bytes=48 * 1024 * 1024
        ),
    )(*(pltpu.with_memory_space_constraint(a, pltpu.HBM) for a in (*fields, *cells)))
    e, h = pl.pallas_call(
        hand_out,
        out_shape=(jax.ShapeDtypeStruct((3, 8, 32, 128), F32),) * 2,
        in_specs=[pl.BlockSpec(memory_space=pltpu.VMEM)] * 2,
        out_specs=(pl.BlockSpec(memory_space=pltpu.HBM),) * 2,
        scratch_shapes=[pltpu.SemaphoreType.DMA((6,))],
    )(*(pltpu.with_memory_space_constraint(a, pltpu.VMEM) for a in (e, h)))
    return e.reshape(3, 64, 4, 128), h.reshape(3, 64, 4, 128)


def solution(mesh):
    field, cell = P(None, None, "gx", "gy"), P(None, "gx", "gy")
    return jax.shard_map(
        shards, mesh=mesh, in_specs=(field,) * 5 + (cell,) * 3, out_specs=(field, field), check_vma=False
    )
```

```python
import contextlib

import jax
import jax.numpy as jnp
from jax import lax
from jax.experimental import pallas as pl
from jax.experimental.pallas import tpu as pltpu
from jax.sharding import PartitionSpec as P

STEPS = 14
BLOCKS = 3
MESH = pl.DeviceIdType.MESH
NAMED = False
F32 = jnp.float32

TILES = 10
TILE = 16
COMP = 12 * TILE
ROWS = 80
OWN = 2
CROSS = 8
ZERO_H = 9
THIRD = 8
FREE = 10
ZERO_E = 14
PLANES = 15

C_J = 0.975 / 1.025
C_E = 2.0 * (1.125 / 1.025)

SLOTS = ["perm", "mat", "abs", "e0", "e1", "e2", "h0", "h1", "h2", "j0", "j1", "j2", "p0", "p1", "p2", "q0", "q1", "q2"]
GROUPS = 5
GHOST = STEPS


def scope(name):
    return jax.named_scope(name) if NAMED else contextlib.nullcontext()


def towards(axis, step):
    count = lax.axis_size(axis)
    return {axis: lax.rem(lax.axis_index(axis) + step + count, count)}


def lanes(rows=8):
    return lax.broadcasted_iota(jnp.int32, (rows, 128), 1)


def loop(low, high, body):
    lax.fori_loop(low, high, lambda i, carry: (body(i), carry)[1], 0)


def loop_by(size, count, body):
    loop(0, count // size, lambda i: [body(size * i + k) for k in range(size)])


def at(c, t, shift=0):
    return pl.ds(COMP * c + TILE * (t + 1) + shift, 8)


def packed(c, t):
    return pl.ds(ROWS * c + 8 * t, 8)


class Tiles:
    def __init__(self, ref, plane):
        self.ref, self.plane, self.held = ref, plane, {}

    def __call__(self, c, t):
        if (c, t) not in self.held:
            self.held[c, t] = self.ref[self.plane, at(c, t)]
        return self.held[c, t]


@contextlib.contextmanager
def later(*stores):
    yield
    for store in stores:
        store()


def pipelined(load, work):
    loaded = load(0)
    for t in range(TILES):
        later = load(t + 1) if t + 1 < TILES else None
        work(t, loaded)
        loaded = later


def h_pass(e, h, ah, bh, src, nxt, dst, cell):
    tile = Tiles(e, src)

    def load(t):
        here = pl.ds(8 * t, 8)
        return (
            [tile(c, t) for c in range(3)],
            tile(0, t + 1), tile(2, t + 1),
            e[src, at(0, t, 1)], e[src, at(1, t, 1)],
            e[nxt, at(1, t)], e[nxt, at(2, t)],
            [h[src, at(c, t)] for c in range(3)],
            ah[cell, here], bh[cell, here],
        )

    def work(t, loaded):
        (ex, ey, ez), ex_y, ez_y, ex_z, ey_z, ey_x, ez_x, (hx, hy, hz), a, b = loaded
        h[dst, at(0, t)] = a * hx - b * ((ez_y - ez) - (ey_z - ey))
        h[dst, at(1, t)] = a * hy - b * ((ex_z - ex) - (ez_x - ez))
        h[dst, at(2, t)] = a * hz - b * ((ey_x - ey) - (ex_y - ex))

    pipelined(load, work)


def e_pass(e, h, j, p, q, ae, be, bm, src, mag, prv, dst, cell):
    tile = Tiles(h, mag)

    def load(t):
        here = pl.ds(8 * t, 8)
        media = [(e[src, at(c, t)], j[src, packed(c, t)], p[src, packed(c, t)], q[src, packed(c, t)]) for c in range(3)]
        return (
            media,
            [tile(c, t) for c in range(3)],
            tile(0, t - 1), tile(2, t - 1),
            h[mag, at(0, t, -1)], h[mag, at(1, t, -1)],
            h[prv, at(1, t)], h[prv, at(2, t)],
            ae[cell, here], be[cell, here], bm[cell, here],
        )

    def work(t, loaded):
        media, (hx, hy, hz), hx_y, hz_y, hx_z, hy_z, hy_x, hz_x, a, b, m = loaded
        curl = (
            (hz - hz_y) - (hy - hy_z),
            (hx - hx_z) - (hz - hz_x),
            (hy - hy_x) - (hx - hx_y),
        )
        for c in range(3):
            ec, jc, pc, qc = media[c]
            jc = C_J * jc + C_E * ec
            qc = 0.9 * qc + (ec - pc)
            pc = pc + 0.25 * qc
            j[dst, packed(c, t)] = jc
            q[dst, packed(c, t)] = qc
            p[dst, packed(c, t)] = pc
            e[dst, at(c, t)] = a * ec + (b * curl[c] - m * (jc + qc))

    pipelined(load, work)


def edges_e(e, plane):
    tiles = [e[plane, at(c, 0)] for c in (0, 2)]
    first = e[plane, pl.ds(0, 24, stride=TILE)]
    tiles = [pltpu.roll(tile, 127, 1) for tile in tiles]
    first = jnp.where(lanes(24) < 112, pltpu.roll(first, 112, 1), 0.0)

    def store():
        e[plane, at(0, TILES)], e[plane, at(2, TILES)] = tiles
        e[plane, pl.ds(8, 24, stride=TILE)] = first

    return store


def edges_h(h, plane):
    tiles = [h[plane, at(c, TILES - 1)] for c in (0, 2)]
    last = h[plane, pl.ds(TILE + 7, 24, stride=TILE)]
    tiles = [pltpu.roll(tile, 1, 1) for tile in tiles]
    last = jnp.where(lanes(24) < 16, 0.0, pltpu.roll(last, 16, 1))

    def store():
        h[plane, at(0, -1)], h[plane, at(2, -1)] = tiles
        h[plane, pl.ds(TILE - 1, 24, stride=TILE)] = last

    return store


def kernel(
    e_in, h_in, j_in, p_in, q_in, perm_in, mat_in, abs_in, e_out, h_out,
    stage, ints, turned, raw, e, h, j, p, q, ah, bh, ae, be, bm, cross,
    send_e, send_h, recv_e, recv_h, in_sem, y_sem, x_sem, s_sem, re_sem, rh_sem,
):
    def blank(zb):
        for g in range(GROUPS):
            for edge in (0, 152):
                turned[g, zb, pl.ds(edge, 8)] = jnp.zeros((8, 128), F32)

    loop(0, 8, blank)

    barrier = pltpu.get_barrier_semaphore()
    for axis in ("gx", "gy"):
        for step in (-1, 1):
            pl.semaphore_signal(barrier, inc=1, device_id=towards(axis, step), device_id_type=MESH)

    fields = (e_in, h_in, j_in, p_in, q_in)
    pltpu.make_async_copy(perm_in, stage.at[0], in_sem.at[0]).start()
    pltpu.make_async_copy(mat_in, ints.at[0], in_sem.at[0]).start()
    pltpu.make_async_copy(abs_in, ints.at[1], in_sem.at[0]).start()
    for i, f in enumerate(fields):
        pltpu.make_async_copy(f, stage.at[pl.ds(3 + 3 * i, 3)], in_sem.at[i]).start()

    def arrive(ref, sem):
        pltpu.make_async_copy(ref, ref, sem).wait()

    def clear(planes, refs):
        for ref in refs:
            size = ref.shape[1] // 6

            def body(i):
                for plane in planes:
                    for k in range(size // 8):
                        ref[plane, pl.ds(pl.multiple_of(size * i + 8 * k, 8), 8)] = jnp.zeros((8, 128), F32)

            loop(0, 6, body)

    clear((ZERO_E,), (e,))
    clear((ZERO_H,), (h,))

    def turn(g):
        slots = range(4 * g, min(4 * g + 4, len(SLOTS)))

        def body(zb):
            rows = []
            for block in (zb,) if g < 4 else (zb, zb + 4):
                for slot in slots:
                    for x in range(4):
                        here = pl.ds(x, 8, stride=4)
                        if slot in (1, 2):
                            rows.append(ints[slot - 1, block, here].astype(F32))
                        else:
                            rows.append(stage[slot, block, here])
            turned[g, zb, pl.ds(16, 128)] = jnp.transpose(jnp.concatenate(rows, 0))

        loop_by(2, 8 if g < 4 else 4, body)

    def columns(g, step):
        source, target = (pl.ds(16, GHOST), pl.ds(144, GHOST)) if step < 0 else (pl.ds(144 - GHOST, GHOST), pl.ds(16 - GHOST, GHOST))
        blocks = pl.ds(0, 8 if g < 4 else 4)
        return pltpu.make_async_remote_copy(
            src_ref=turned.at[g, blocks, source], dst_ref=turned.at[g, blocks, target],
            send_sem=y_sem.at[GROUPS], recv_sem=y_sem.at[g],
            device_id=towards("gy", step), device_id_type=MESH,
        )

    for g in range(GROUPS):
        with scope("turn"):
            if g < 4:
                arrive(stage.at[pl.ds(0, 6)] if g == 0 else stage.at[pl.ds(3 + 3 * g, 3)], in_sem.at[g])
            if g == 3:
                arrive(stage.at[pl.ds(15, 3)], in_sem.at[4])
            turn(g)
        if g == 0:
            with scope("barrier"):
                pl.semaphore_wait(barrier, 4)
        for step in (-1, 1):
            columns(g, step).start()

    state = {"e": e, "h": h, "j": j, "p": p, "q": q}

    def build(g):
        def body(t):
            rows = jnp.concatenate([turned[g, zb, pl.ds(t, 16, stride=10)] for zb in range(8 if g < 4 else 4)], 0)
            if g == 4:
                rows = jnp.concatenate([rows, pltpu.roll(rows, 64, 1)], 0)
                rows = rows[:, :64]
            whole = jnp.transpose(rows)
            for s, name in enumerate(SLOTS[4 * g : 4 * g + 4]):
                for x in range(4):
                    part = whole[32 * s + 8 * x : 32 * s + 8 * x + 8]
                    if 4 * g + s < 3:
                        raw[OWN + x, 4 * g + s, pl.ds(pl.multiple_of(8 * t, 8), 8)] = part
                        continue
                    c = int(name[1])
                    if name[0] in "eh":
                        row = COMP * c + TILE * (t + 1)
                    else:
                        row = ROWS * c + 8 * t
                    if name[0] in "jq":
                        part = part * 2.0
                    state[name[0]][OWN + x, pl.ds(pl.multiple_of(row, 8), 8)] = part

        loop_by(2 if g < 4 else 5, TILES, body)

    def layer(source, target, step, k):
        return pltpu.make_async_remote_copy(
            src_ref=source, dst_ref=target, send_sem=x_sem.at[3], recv_sem=x_sem.at[k],
            device_id=towards("gx", step), device_id_type=MESH,
        )

    def coefficients(plane, h_alone=False):
        for t in range(TILES):
            here = pl.ds(8 * t, 8)
            s = 0.1 * raw[plane, 2, here]
            r = 1.0 / (1.0 + s)
            ah[plane, here] = (1.0 - s) * r
            bh[plane, here] = 0.5 * r
            if h_alone:
                continue
            perm, mat = raw[plane, 0, here], raw[plane, 1, here]
            eff = jnp.where(mat == 0.0, 1.0, perm)
            se = s / eff
            r = 1.0 / (1.0 + se)
            ae[plane, here] = (1.0 - se) * r
            b = 0.5 * r / eff
            be[plane, here] = b
            bm[plane, here] = jnp.where(mat == 2.0, 0.5 * b, 0.0)

    def trace_e(step, mark):
        return pltpu.make_async_remote_copy(
            src_ref=send_e.at[step], dst_ref=recv_e.at[step],
            send_sem=s_sem.at[0], recv_sem=re_sem.at[mark],
            device_id=towards("gx", -1), device_id_type=MESH,
        )

    def trace_h(step, mark):
        return pltpu.make_async_remote_copy(
            src_ref=send_h.at[step], dst_ref=recv_h.at[step],
            send_sem=s_sem.at[1], recv_sem=rh_sem.at[mark],
            device_id=towards("gx", 1), device_id_type=MESH,
        )

    def give(ref, plane, out, step):
        for c in range(2):
            for t in range(TILES):
                out[step, c, pl.ds(8 * t, 8)] = ref[plane, at(1 + c, t)]

    def take(ref, plane, trace, step):
        for c in range(2):
            for t in range(TILES):
                ref[CROSS, at(1 + c, t)] = ref[plane, at(1 + c, t)] + trace[step, c, pl.ds(8 * t, 8)]

    def free_h(x, src, dst):
        nxt = src + x + 1 + (x // 3) * (ZERO_E - src - 4)
        h_pass(e, h, ah, bh, src + x, nxt, dst + x, OWN + x)

    def free_e(x, src, dst):
        prv = dst + x - 1 + (1 - (x + 2) // 3) * (ZERO_H - dst + 1)
        e_pass(e, h, j, p, q, ae, be, bm, src + x, dst + x, prv, dst + x, OWN + x)

    def give_e(plane, step, mark):
        give(e, plane, send_e, step)
        trace_e(step, mark).start()

    def give_h(plane, step, mark):
        give(h, plane, send_h, step)
        trace_h(step, mark).start()

    def h_part(src, dst, step, mark):
        give_e(src, step, mark)
        with later(*(edges_e(e, src + x) for x in range(3))):
            free_h(3, src, dst)
        give_h(dst + 3, step, mark)
        with later(edges_h(h, dst + 3)):
            free_h(0, src, dst)
            free_h(1, src, dst)
            free_h(2, src, dst)

    for g in range(GROUPS):
        with scope("ghosts"):
            arrive(turned.at[g, pl.ds(0, 8 if g < 4 else 4), pl.ds(0, 2 * GHOST)], y_sem.at[g])
        with scope("build"):
            build(g)
        if g == 0:
            layer(raw.at[OWN], raw.at[OWN + 4], -1, 0).start()
            layer(raw.at[OWN + 3], raw.at[OWN - 1], 1, 0).start()
            layer(raw.at[OWN + 2, 2], raw.at[OWN - 2, 2], 1, 1).start()
            loop(OWN, OWN + 4, coefficients)
        if g == 1:
            loop(OWN, OWN + 4, lambda x: edges_e(e, x)())
        if g == 2:
            h_part(OWN, OWN, 0, 0)
            layer(be.at[OWN + 1], be.at[OWN + 5], -1, 2).start()
            layer(be.at[OWN + 2], be.at[OWN - 2], 1, 2).start()
            ah[OWN + 5] = jnp.zeros((ROWS, 128), F32)
            for t in range(TILES):
                here = pl.ds(8 * t, 8)
                product = be[OWN, here] * bh[OWN, here]
                for x in range(1, 4):
                    product = product * (be[OWN + x, here] * bh[OWN + x, here])
                cross[here] = product

    def block(b, carry):
        size = 4 + (b + 1) // 2
        start = 4 * b + b // 2
        far = size // 5
        marks = 5 * lax.rem(b, 2) - start

        def free(i):
            src = OWN + (i // 2) * (FREE - OWN)
            dst = OWN + ((i + 3) // 4) * (FREE - OWN)
            last = (i + 2) // size
            loop(1 - (i + 3) // 4, 1, lambda _: h_part(src, dst, start + i, marks + start + i))
            with later(edges_h(h, dst)):
                free_e(3, src, dst)
            with later(edges_e(e, dst + 3), edges_h(h, dst + 1), edges_h(h, dst + 2)):
                free_e(0, src, dst)

            def inner(_):
                free_e(1, src, dst)
                free_e(2, src, dst)

            loop(last, 1, inner)

        with scope("free"):
            loop(0, size - 1, free)
            end = start + size - 1
            free_h(3, FREE, FREE)

            def give_last(_):
                give_e(FREE, end, marks + end)
                give_h(FREE + 3, end, marks + end)

            loop(far, 1, give_last)

            def more_layers(_):
                for ref in (ae, bm):
                    layer(ref.at[OWN + 1], ref.at[OWN + 5], -1, 4).start()
                    layer(ref.at[OWN + 2], ref.at[OWN - 2], 1, 4).start()
                layer(bh.at[OWN + 1], bh.at[OWN + 5], -1, 4).start()
                layer(bh.at[OWN + 1], bh.at[THIRD], 1, 4).start()

            loop((b + 3) // 4, 1, more_layers)

        with scope("clear"):
            clear((0, 1, 6, 7), (e, h))
            clear((0, 1, 6, 7), (j, p, q))

        def ghost_coefficients(_):
            arrive(raw.at[pl.ds(0, 2)], x_sem.at[0])
            coefficients(1)
            coefficients(6)
            arrive(raw.at[0, 2], x_sem.at[1])
            coefficients(0, h_alone=True)
            arrive(be.at[pl.ds(0, 2)], x_sem.at[2])

        with scope("ghostcoef"):
            loop((b + 3) // 4, 1, ghost_coefficients)
            loop(1 - b * (1 - b // 2), 1, lambda _: arrive(be.at[pl.ds(0, 6)], x_sem.at[4]))

        def from_own(cell, mag, plane):
            for t in range(TILES):
                b = be[cell, pl.ds(8 * t, 8)]
                hy, hz = h[mag, at(1, t)], h[mag, at(2, t)]
                curl = (hz - h[mag, at(2, t - 1)]) - (hy - h[mag, at(1, t, -1)])
                e[plane, at(0, t)] = e[plane, at(0, t)] + b * curl
                e[plane, at(1, t)] = e[plane, at(1, t)] - b * hz
                e[plane, at(2, t)] = e[plane, at(2, t)] + b * hy

        def from_below(mag, plane):
            for t in range(TILES):
                b = be[plane, pl.ds(8 * t, 8)]
                e[plane, at(1, t)] = b * h[mag, at(2, t)]
                e[plane, at(2, t)] = -b * h[mag, at(1, t)]

        def answer(trace, cell, delta, plane):
            for t in range(TILES):
                here = pl.ds(8 * t, 8)
                b = bh[cell, here]
                hy, hz = b * trace[start, 1, here], b * trace[start, 0, here]
                h[delta, at(1, t)] = hy
                h[delta, at(2, t)] = -hz
                if delta != plane:
                    h[plane, at(1, t)] = h[plane, at(1, t)] + hy
                    h[plane, at(2, t)] = h[plane, at(2, t)] - hz
            edges_h(h, delta)()
            from_own(cell, delta, plane)

        with scope("first"):
            answer(send_e, 1, 1, 1)
            def passed_h(_):
                trace_h(start, marks + start).wait_recv()

                def give_last(_):
                    for c in range(2):
                        for t in range(TILES):
                            here = pl.ds(8 * t, 8)
                            below = h[1, at(1 + c, t)] + recv_h[start, c, here]
                            send_h[end, c, here] = h[FREE + 3, at(1 + c, t)] + cross[here] * below
                    trace_h(end, marks + end).start()

                loop(1 - far, 1, give_last)

            def passed_e(_):
                for c in range(2):
                    for t in range(TILES):
                        here = pl.ds(8 * t, 8)
                        send_e[end, c, here] = e[FREE, at(1 + c, t)] + cross[here] * recv_e[start, c, here]
                trace_e(end, marks + end).start()

            odd = lax.rem(lax.axis_index("gx"), 2)
            loop(1 - odd, 1, passed_h)
            with scope("wait_e"):
                trace_e(start, marks + start).wait_recv()
            loop(1 - far, 1, passed_e)
            answer(recv_e, 5, FREE + 1, 5)
            from_below(5, 6)
            with scope("wait_h"):
                loop(odd, 1, passed_h)
            for t in range(TILES):
                here = pl.ds(8 * t, 8)
                own = be[2, here]
                e[2, at(1, t)] = e[2, at(1, t)] + own * (h[1, at(2, t)] + recv_h[start, 1, here])
                e[2, at(2, t)] = e[2, at(2, t)] - own * (h[1, at(1, t)] + recv_h[start, 0, here])

        def true(i):
            step = start + i
            final = (i + 1) // size
            deep = 1 - i // 2
            wide = far * (i // 2) * (1 - i // 3)

            def true_h(x, nxt):
                h_pass(e, h, ah, bh, x, nxt, x, x)

            def true_e(x, prv):
                e_pass(e, h, j, p, q, ae, be, bm, x, x, prv, x, x)

            with later(*(edges_e(e, x) for x in (0, 1, 2, 5, 6, 7))):
                true_h(3, 4)
                true_h(4, 5)
            with later(edges_h(h, 3), edges_h(h, 4)):
                true_h(1, 2)
                true_h(2, 3)
            loop(final, 1, lambda _: true_h(0, 1))
            with later(edges_h(h, 0), edges_h(h, 1), edges_h(h, 2)):
                true_e(3, 2)
                true_e(4, 3)
            loop(final, 1, lambda _: true_e(1, 0))
            with scope("wait_e"):
                trace_e(step, marks + step).wait_recv()
            take(e, 6, recv_e, step)
            with later(edges_e(e, 3), edges_e(e, 4)):
                true_h(5, CROSS)
            loop(final, 1, lambda _: true_h(6, 7))

            def wide_h(_):
                true_h(7, ZERO_E)
                for t in range(TILES):
                    b = bh[THIRD, pl.ds(8 * t, 8)]
                    h[FREE, at(1, t)] = b * e[0, at(2, t)]
                    h[FREE, at(2, t)] = -b * e[0, at(1, t)]
                edges_h(h, 7)()

            loop(1 - wide, 1, wide_h)
            for store in (edges_h(h, 5), edges_h(h, 6)):
                store()
            true_e(5, 4)
            loop(final, 1, lambda _: true_e(6, 5))
            loop(1 - deep, 1, lambda _: from_below(6, 7))
            with scope("wait_h"):
                trace_h(step, marks + step).wait_recv()
            take(h, 1, recv_h, step)
            with later(edges_e(e, 5)):
                true_e(2, CROSS)
            loop(1 - deep, 1, lambda _: from_own(0, 0, 0))

            def wide_e(_):
                true_e(7, 6)
                true_e(0, FREE)

            loop(1 - wide, 1, wide_e)

        with scope("true"):
            loop(1, size, true)

        def onward(_):
            h_part(OWN, OWN, start + size, 5 * lax.rem(b + 1, 2))

        loop(b // 2, 1, onward)
        return carry

    lax.fori_loop(0, BLOCKS, block, 0)

    with scope("finish"):
        arrive(send_e, s_sem.at[0])
        arrive(send_h, s_sem.at[1])
        arrive(raw.at[pl.ds(0, 5)], x_sem.at[3])
        arrive(turned.at[0, :, pl.ds(0, 9 * GHOST)], y_sem.at[GROUPS])

    results = [(e, c) for c in range(3)] + [(h, c) for c in range(3)]
    outs = [(e_out, c) for c in range(3)] + [(h_out, c) for c in range(3)]
    with scope("results"):
        def gather(t):
            for g in range(2):
                group = results[4 * g : 4 * g + 4]
                tiles = [ref[OWN + x, pl.ds(pl.multiple_of(COMP * c + TILE * (t + 1), 8), 8)] for ref, c in group for x in range(4)]
                tiles = jnp.concatenate(tiles, 0)
                if g == 1:
                    tiles = jnp.concatenate([tiles, pltpu.roll(tiles, 64, 1)], 0)[:, :64]
                whole = jnp.transpose(tiles)
                for zb in range(8 if g == 0 else 4):
                    turned[g, zb, pl.ds(t, 16, stride=10)] = whole[16 * zb : 16 * zb + 16]

        loop_by(2, TILES, gather)

        def spread(g, zb):
            whole = jnp.transpose(turned[g, zb, pl.ds(16, 128)])
            group = outs[4 * g : 4 * g + 4]
            row = 0
            for block in (zb,) if g == 0 else (zb, zb + 4):
                for out, c in group:
                    for x in range(4):
                        out[c, block, pl.ds(x, 8, stride=4)] = whole[row : row + 8]
                        row += 8

        loop(0, 4, lambda zb: (spread(0, 2 * zb), spread(0, 2 * zb + 1), spread(1, zb)))


def hand_out(e, h, e_out, h_out, sem):
    copies = [
        pltpu.make_async_copy(ref.at[c], out.at[c], sem.at[3 * i + c])
        for i, (ref, out) in enumerate(((e, e_out), (h, h_out)))
        for c in range(3)
    ]
    for copy in copies:
        copy.start()
    for copy in copies:
        copy.wait()


def shards(
    e_field, h_field, drude_current, lorentz_polar, lorentz_rate, permittivity, material, absorber
):
    fields = [f.reshape(3, 8, 32, 128) for f in (e_field, h_field, drude_current, lorentz_polar, lorentz_rate)]
    cells = [c.reshape(8, 32, 128) for c in (permittivity, material, absorber)]
    wide = pltpu.VMEM((PLANES, 3 * COMP, 128), F32)
    narrow = pltpu.VMEM((PLANES, 3 * ROWS, 128), F32)
    cell = pltpu.VMEM((9, ROWS, 128), F32)
    trace = pltpu.VMEM((STEPS, 2, ROWS, 128), F32)
    e, h = pl.pallas_call(
        kernel,
        out_shape=(pltpu.VMEM((3, 8, 32, 128), F32),) * 2,
        in_specs=[pl.BlockSpec(memory_space=pl.ANY)] * 8,
        out_specs=(pl.BlockSpec(memory_space=pltpu.VMEM),) * 2,
        scratch_shapes=[
            pltpu.VMEM((18, 8, 32, 128), F32),
            pltpu.VMEM((2, 8, 32, 128), jnp.int32),
            pltpu.VMEM((GROUPS, 8, 160, 128), F32),
            pltpu.VMEM((8, 3, ROWS, 128), F32),
            wide, wide, narrow, narrow, narrow,
            cell, cell, cell, cell, cell, pltpu.VMEM((ROWS, 128), F32),
            trace, trace, trace, trace,
            pltpu.SemaphoreType.DMA((5,)),
            pltpu.SemaphoreType.DMA((GROUPS + 1,)),
            pltpu.SemaphoreType.DMA((5,)),
            pltpu.SemaphoreType.DMA((2,)),
            pltpu.SemaphoreType.DMA((10,)),
            pltpu.SemaphoreType.DMA((10,)),
        ],
        compiler_params=pltpu.CompilerParams(
            collective_id=0, has_side_effects=True, vmem_limit_bytes=48 * 1024 * 1024
        ),
    )(*(pltpu.with_memory_space_constraint(a, pltpu.HBM) for a in (*fields, *cells)))
    e, h = pl.pallas_call(
        hand_out,
        out_shape=(jax.ShapeDtypeStruct((3, 8, 32, 128), F32),) * 2,
        in_specs=[pl.BlockSpec(memory_space=pltpu.VMEM)] * 2,
        out_specs=(pl.BlockSpec(memory_space=pltpu.HBM),) * 2,
        scratch_shapes=[pltpu.SemaphoreType.DMA((6,))],
    )(*(pltpu.with_memory_space_constraint(a, pltpu.VMEM) for a in (e, h)))
    return e.reshape(3, 64, 4, 128), h.reshape(3, 64, 4, 128)


def solution(mesh):
    field, cell = P(None, None, "gx", "gy"), P(None, "gx", "gy")
    return jax.shard_map(
        shards, mesh=mesh, in_specs=(field,) * 5 + (cell,) * 3, out_specs=(field, field), check_vma=False
    )
```

```python
import contextlib

import jax
import jax.numpy as jnp
from jax import lax
from jax.experimental import pallas as pl
from jax.experimental.pallas import tpu as pltpu
from jax.sharding import PartitionSpec as P

STEPS = 14
BLOCKS = 3
MESH = pl.DeviceIdType.MESH
NAMED = False
F32 = jnp.float32

TILES = 10
TILE = 16
COMP = 12 * TILE
ROWS = 80
OWN = 2
CROSS = 8
ZERO_H = 9
THIRD = 8
FREE = 10
ZERO_E = 14
PLANES = 15

C_J = 0.975 / 1.025
C_E = 2.0 * (1.125 / 1.025)

SLOTS = ["perm", "mat", "abs", "e0", "e1", "e2", "h0", "h1", "h2", "j0", "j1", "j2", "p0", "p1", "p2", "q0", "q1", "q2"]
GROUPS = 5
BELOW = (14, 14, 14, 13, 13)
ABOVE = (14, 14, 13, 13, 13)


def scope(name):
    return jax.named_scope(name) if NAMED else contextlib.nullcontext()


def towards(axis, step):
    count = lax.axis_size(axis)
    return {axis: lax.rem(lax.axis_index(axis) + step + count, count)}


def lanes(rows=8):
    return lax.broadcasted_iota(jnp.int32, (rows, 128), 1)


def loop(low, high, body):
    lax.fori_loop(low, high, lambda i, carry: (body(i), carry)[1], 0)


def loop_by(size, count, body):
    loop(0, count // size, lambda i: [body(size * i + k) for k in range(size)])


def at(c, t, shift=0):
    return pl.ds(COMP * c + TILE * (t + 1) + shift, 8)


def packed(c, t):
    return pl.ds(ROWS * c + 8 * t, 8)


class Tiles:
    def __init__(self, ref, plane):
        self.ref, self.plane, self.held = ref, plane, {}

    def __call__(self, c, t):
        if (c, t) not in self.held:
            self.held[c, t] = self.ref[self.plane, at(c, t)]
        return self.held[c, t]


@contextlib.contextmanager
def later(*stores):
    yield
    for store in stores:
        store()


def pipelined(load, work):
    loaded = load(0)
    for t in range(TILES):
        later = load(t + 1) if t + 1 < TILES else None
        work(t, loaded)
        loaded = later


def h_pass(e, h, ah, bh, src, nxt, dst, cell):
    tile = Tiles(e, src)

    def load(t):
        here = pl.ds(8 * t, 8)
        return (
            [tile(c, t) for c in range(3)],
            tile(0, t + 1), tile(2, t + 1),
            e[src, at(0, t, 1)], e[src, at(1, t, 1)],
            e[nxt, at(1, t)], e[nxt, at(2, t)],
            [h[src, at(c, t)] for c in range(3)],
            ah[cell, here], bh[cell, here],
        )

    def work(t, loaded):
        (ex, ey, ez), ex_y, ez_y, ex_z, ey_z, ey_x, ez_x, (hx, hy, hz), a, b = loaded
        h[dst, at(0, t)] = a * hx - b * ((ez_y - ez) - (ey_z - ey))
        h[dst, at(1, t)] = a * hy - b * ((ex_z - ex) - (ez_x - ez))
        h[dst, at(2, t)] = a * hz - b * ((ey_x - ey) - (ex_y - ex))

    pipelined(load, work)


def e_pass(e, h, j, p, q, ae, be, bm, src, mag, prv, dst, cell):
    tile = Tiles(h, mag)

    def load(t):
        here = pl.ds(8 * t, 8)
        media = [(e[src, at(c, t)], j[src, packed(c, t)], p[src, packed(c, t)], q[src, packed(c, t)]) for c in range(3)]
        return (
            media,
            [tile(c, t) for c in range(3)],
            tile(0, t - 1), tile(2, t - 1),
            h[mag, at(0, t, -1)], h[mag, at(1, t, -1)],
            h[prv, at(1, t)], h[prv, at(2, t)],
            ae[cell, here], be[cell, here], bm[cell, here],
        )

    def work(t, loaded):
        media, (hx, hy, hz), hx_y, hz_y, hx_z, hy_z, hy_x, hz_x, a, b, m = loaded
        curl = (
            (hz - hz_y) - (hy - hy_z),
            (hx - hx_z) - (hz - hz_x),
            (hy - hy_x) - (hx - hx_y),
        )
        for c in range(3):
            ec, jc, pc, qc = media[c]
            jc = C_J * jc + C_E * ec
            qc = 0.9 * qc + (ec - pc)
            pc = pc + 0.25 * qc
            j[dst, packed(c, t)] = jc
            q[dst, packed(c, t)] = qc
            p[dst, packed(c, t)] = pc
            e[dst, at(c, t)] = a * ec + (b * curl[c] - m * (jc + qc))

    pipelined(load, work)


def edges_e(e, plane):
    tiles = [e[plane, at(c, 0)] for c in (0, 2)]
    first = e[plane, pl.ds(0, 24, stride=TILE)]
    tiles = [pltpu.roll(tile, 127, 1) for tile in tiles]
    first = jnp.where(lanes(24) < 112, pltpu.roll(first, 112, 1), 0.0)

    def store():
        e[plane, at(0, TILES)], e[plane, at(2, TILES)] = tiles
        e[plane, pl.ds(8, 24, stride=TILE)] = first

    return store


def edges_h(h, plane):
    tiles = [h[plane, at(c, TILES - 1)] for c in (0, 2)]
    last = h[plane, pl.ds(TILE + 7, 24, stride=TILE)]
    tiles = [pltpu.roll(tile, 1, 1) for tile in tiles]
    last = jnp.where(lanes(24) < 16, 0.0, pltpu.roll(last, 16, 1))

    def store():
        h[plane, at(0, -1)], h[plane, at(2, -1)] = tiles
        h[plane, pl.ds(TILE - 1, 24, stride=TILE)] = last

    return store


def kernel(
    e_in, h_in, j_in, p_in, q_in, perm_in, mat_in, abs_in, e_out, h_out,
    stage, ints, turned, raw, e, h, j, p, q, ah, bh, ae, be, bm, cross,
    send_e, send_h, recv_e, recv_h, in_sem, y_sem, x_sem, s_sem, re_sem, rh_sem,
):
    fields = (e_in, h_in, j_in, p_in, q_in)
    pltpu.make_async_copy(perm_in, stage.at[0], in_sem.at[0]).start()
    pltpu.make_async_copy(mat_in, ints.at[0], in_sem.at[0]).start()
    pltpu.make_async_copy(abs_in, ints.at[1], in_sem.at[0]).start()
    pltpu.make_async_copy(e_in.at[0], stage.at[3], in_sem.at[0]).start()
    pltpu.make_async_copy(e_in.at[pl.ds(1, 2)], stage.at[pl.ds(4, 2)], in_sem.at[1]).start()
    for i, f in enumerate(fields[1:], 1):
        pltpu.make_async_copy(f, stage.at[pl.ds(3 + 3 * i, 3)], in_sem.at[i]).start()

    def blank(zb):
        for g in range(GROUPS):
            for edge in (0, 152):
                turned[g, zb, pl.ds(edge, 8)] = jnp.zeros((8, 128), F32)

    loop(0, 8, blank)

    barrier = pltpu.get_barrier_semaphore()
    for axis in ("gx", "gy"):
        for step in (-1, 1):
            pl.semaphore_signal(barrier, inc=1, device_id=towards(axis, step), device_id_type=MESH)

    def arrive(ref, sem):
        pltpu.make_async_copy(ref, ref, sem).wait()

    def clear(planes, refs):
        for ref in refs:
            size = ref.shape[1] // 6

            def body(i):
                for plane in planes:
                    for k in range(size // 8):
                        ref[plane, pl.ds(pl.multiple_of(size * i + 8 * k, 8), 8)] = jnp.zeros((8, 128), F32)

            loop(0, 6, body)

    clear((ZERO_E,), (e,))
    clear((ZERO_H,), (h,))

    def turn(g):
        slots = range(4 * g, min(4 * g + 4, len(SLOTS)))

        def body(zb):
            rows = []
            for block in (zb,) if g < 4 else (zb, zb + 4):
                for slot in slots:
                    for x in range(4):
                        here = pl.ds(x, 8, stride=4)
                        if slot in (1, 2):
                            rows.append(ints[slot - 1, block, here].astype(F32))
                        else:
                            rows.append(stage[slot, block, here])
            turned[g, zb, pl.ds(16, 128)] = jnp.transpose(jnp.concatenate(rows, 0))

        loop_by(2, 8 if g < 4 else 4, body)

    def columns(g, step):
        count = ABOVE[g] if step < 0 else BELOW[g]
        source, target = (16, 144) if step < 0 else (144 - count, 16 - count)
        source, target = pl.ds(source, count), pl.ds(target, count)
        blocks = pl.ds(0, 8 if g < 4 else 4)
        return pltpu.make_async_remote_copy(
            src_ref=turned.at[g, blocks, source], dst_ref=turned.at[g, blocks, target],
            send_sem=y_sem.at[GROUPS], recv_sem=y_sem.at[g],
            device_id=towards("gy", step), device_id_type=MESH,
        )

    for g in range(GROUPS):
        with scope("turn"):
            if g < 4:
                arrive(stage.at[(pl.ds(0, 4), pl.ds(4, 5), pl.ds(9, 3), pl.ds(12, 3))[g]], in_sem.at[g])
            if g == 3:
                arrive(stage.at[pl.ds(15, 3)], in_sem.at[4])
            turn(g)
        if g == 0:
            with scope("barrier"):
                pl.semaphore_wait(barrier, 4)
        for step in (-1, 1):
            columns(g, step).start()

    state = {"e": e, "h": h, "j": j, "p": p, "q": q}

    def build(g):
        def body(t):
            rows = jnp.concatenate([turned[g, zb, pl.ds(t, 16, stride=10)] for zb in range(8 if g < 4 else 4)], 0)
            if g == 4:
                rows = jnp.concatenate([rows, pltpu.roll(rows, 64, 1)], 0)
                rows = rows[:, :64]
            whole = jnp.transpose(rows)
            for s, name in enumerate(SLOTS[4 * g : 4 * g + 4]):
                for x in range(4):
                    part = whole[32 * s + 8 * x : 32 * s + 8 * x + 8]
                    if 4 * g + s < 3:
                        raw[OWN + x, 4 * g + s, pl.ds(pl.multiple_of(8 * t, 8), 8)] = part
                        continue
                    c = int(name[1])
                    if name[0] in "eh":
                        row = COMP * c + TILE * (t + 1)
                    else:
                        row = ROWS * c + 8 * t
                    if name[0] in "jq":
                        part = part * 2.0
                    state[name[0]][OWN + x, pl.ds(pl.multiple_of(row, 8), 8)] = part

        loop_by(2 if g < 4 else 5, TILES, body)

    def layer(source, target, step, k):
        return pltpu.make_async_remote_copy(
            src_ref=source, dst_ref=target, send_sem=x_sem.at[3], recv_sem=x_sem.at[k],
            device_id=towards("gx", step), device_id_type=MESH,
        )

    def coefficients(plane, h_alone=False):
        for t in range(TILES):
            here = pl.ds(8 * t, 8)
            s = 0.1 * raw[plane, 2, here]
            r = 1.0 / (1.0 + s)
            ah[plane, here] = (1.0 - s) * r
            bh[plane, here] = 0.5 * r
            if h_alone:
                continue
            perm, mat = raw[plane, 0, here], raw[plane, 1, here]
            eff = jnp.where(mat == 0.0, 1.0, perm)
            se = s / eff
            r = 1.0 / (1.0 + se)
            ae[plane, here] = (1.0 - se) * r
            b = 0.5 * r / eff
            be[plane, here] = b
            bm[plane, here] = jnp.where(mat == 2.0, 0.5 * b, 0.0)

    def trace_e(step, mark):
        return pltpu.make_async_remote_copy(
            src_ref=send_e.at[step], dst_ref=recv_e.at[step],
            send_sem=s_sem.at[0], recv_sem=re_sem.at[mark],
            device_id=towards("gx", -1), device_id_type=MESH,
        )

    def trace_h(step, mark):
        return pltpu.make_async_remote_copy(
            src_ref=send_h.at[step], dst_ref=recv_h.at[step],
            send_sem=s_sem.at[1], recv_sem=rh_sem.at[mark],
            device_id=towards("gx", 1), device_id_type=MESH,
        )

    def give(ref, plane, out, step):
        for c in range(2):
            for t in range(TILES):
                out[step, c, pl.ds(8 * t, 8)] = ref[plane, at(1 + c, t)]

    def take(ref, plane, trace, step):
        for c in range(2):
            for t in range(TILES):
                ref[CROSS, at(1 + c, t)] = ref[plane, at(1 + c, t)] + trace[step, c, pl.ds(8 * t, 8)]

    def free_h(x, src, dst):
        nxt = src + x + 1 + (x // 3) * (ZERO_E - src - 4)
        h_pass(e, h, ah, bh, src + x, nxt, dst + x, OWN + x)

    def free_e(x, src, dst):
        prv = dst + x - 1 + (1 - (x + 2) // 3) * (ZERO_H - dst + 1)
        e_pass(e, h, j, p, q, ae, be, bm, src + x, dst + x, prv, dst + x, OWN + x)

    def give_e(plane, step, mark):
        give(e, plane, send_e, step)
        trace_e(step, mark).start()

    def give_h(plane, step, mark):
        give(h, plane, send_h, step)
        trace_h(step, mark).start()

    def h_part(src, dst, step, mark):
        with later(*(edges_e(e, src + x) for x in range(3))):
            free_h(3, src, dst)
        give_h(dst + 3, step, mark)
        with later(edges_h(h, dst + 3)):
            free_h(0, src, dst)
            free_h(1, src, dst)
            free_h(2, src, dst)

    for g in range(GROUPS):
        with scope("ghosts"):
            arrive(turned.at[g, pl.ds(0, 8 if g < 4 else 4), pl.ds(0, BELOW[g] + ABOVE[g])], y_sem.at[g])
        with scope("build"):
            build(g)
        if g == 0:
            layer(raw.at[OWN], raw.at[OWN + 4], -1, 0).start()
            layer(raw.at[OWN + 3], raw.at[OWN - 1], 1, 0).start()
            layer(raw.at[OWN + 2, 2], raw.at[OWN - 2, 2], 1, 1).start()
            loop(OWN, OWN + 4, coefficients)
        if g == 1:
            loop(OWN, OWN + 4, lambda x: edges_e(e, x)())
        if g == 2:
            give_e(OWN, 0, 0)
            h_part(OWN, OWN, 0, 0)
            layer(be.at[OWN + 1], be.at[OWN + 5], -1, 2).start()
            layer(be.at[OWN + 2], be.at[OWN - 2], 1, 2).start()
            ah[OWN + 5] = jnp.zeros((ROWS, 128), F32)
            for t in range(TILES):
                here = pl.ds(8 * t, 8)
                product = be[OWN, here] * bh[OWN, here]
                for x in range(1, 4):
                    product = product * (be[OWN + x, here] * bh[OWN + x, here])
                cross[here] = product

    def block(b, carry):
        size = 4 + (b + 1) // 2
        start = 4 * b + b // 2
        far = size // 5
        marks = 5 * lax.rem(b, 2) - start

        def free(i):
            src = OWN + (i // 2) * (FREE - OWN)
            dst = OWN + ((i + 3) // 4) * (FREE - OWN)
            last = (i + 2) // size
            loop(1 - (i + 3) // 4, 1, lambda _: h_part(src, dst, start + i, marks + start + i))
            with later(edges_h(h, dst)):
                free_e(3, src, dst)
            with later(edges_e(e, dst + 3), edges_h(h, dst + 1), edges_h(h, dst + 2)):
                free_e(0, src, dst)
            loop(last * far, 1, lambda _: give_e(dst, start + i + 1, marks + start + i + 1))

            def inner(_):
                free_e(1, src, dst)
                free_e(2, src, dst)

            loop(last, 1, inner)

        with scope("free"):
            loop(0, size - 1, free)
            end = start + size - 1
            free_h(3, FREE, FREE)

            loop(far, 1, lambda _: give_h(FREE + 3, end, marks + end))

            def more_layers(_):
                for ref in (ae, bm):
                    layer(ref.at[OWN + 1], ref.at[OWN + 5], -1, 4).start()
                    layer(ref.at[OWN + 2], ref.at[OWN - 2], 1, 4).start()
                layer(bh.at[OWN + 1], bh.at[OWN + 5], -1, 4).start()
                layer(bh.at[OWN + 1], bh.at[THIRD], 1, 4).start()

            loop((b + 3) // 4, 1, more_layers)

        with scope("clear"):
            clear((0, 1, 6, 7), (e, h))
            clear((0, 1, 6, 7), (j, p, q))

        def ghost_coefficients(_):
            arrive(raw.at[pl.ds(0, 2)], x_sem.at[0])
            coefficients(1)
            coefficients(6)
            arrive(raw.at[0, 2], x_sem.at[1])
            coefficients(0, h_alone=True)

        with scope("ghostcoef"):
            loop((b + 3) // 4, 1, ghost_coefficients)
            loop(1 - b * (1 - b // 2), 1, lambda _: arrive(be.at[pl.ds(0, 6)], x_sem.at[4]))

        def from_own(cell, mag, plane):
            for t in range(TILES):
                b = be[cell, pl.ds(8 * t, 8)]
                hy, hz = h[mag, at(1, t)], h[mag, at(2, t)]
                curl = (hz - h[mag, at(2, t - 1)]) - (hy - h[mag, at(1, t, -1)])
                e[plane, at(0, t)] = e[plane, at(0, t)] + b * curl
                e[plane, at(1, t)] = e[plane, at(1, t)] - b * hz
                e[plane, at(2, t)] = e[plane, at(2, t)] + b * hy

        def from_below(mag, plane):
            for t in range(TILES):
                b = be[plane, pl.ds(8 * t, 8)]
                e[plane, at(1, t)] = b * h[mag, at(2, t)]
                e[plane, at(2, t)] = -b * h[mag, at(1, t)]

        def answer(trace, cell, delta, plane):
            for t in range(TILES):
                here = pl.ds(8 * t, 8)
                b = bh[cell, here]
                hy, hz = b * trace[start, 1, here], b * trace[start, 0, here]
                h[delta, at(1, t)] = hy
                h[delta, at(2, t)] = -hz
                if delta != plane:
                    h[plane, at(1, t)] = h[plane, at(1, t)] + hy
                    h[plane, at(2, t)] = h[plane, at(2, t)] - hz
            edges_h(h, delta)()
            from_own(cell, delta, plane)

        with scope("first"):
            answer(send_e, 1, 1, 1)
            def passed_h(_):
                trace_h(start, marks + start).wait_recv()

                def give_last(_):
                    for c in range(2):
                        for t in range(TILES):
                            here = pl.ds(8 * t, 8)
                            below = h[1, at(1 + c, t)] + recv_h[start, c, here]
                            send_h[end, c, here] = h[FREE + 3, at(1 + c, t)] + cross[here] * below
                    trace_h(end, marks + end).start()

                loop(1 - far, 1, give_last)

            def passed_e(_):
                for c in range(2):
                    for t in range(TILES):
                        here = pl.ds(8 * t, 8)
                        send_e[end, c, here] = e[FREE, at(1 + c, t)] + cross[here] * recv_e[start, c, here]
                trace_e(end, marks + end).start()

            odd = lax.rem(lax.axis_index("gx"), 2)
            loop(1 - odd, 1, passed_h)
            with scope("wait_e"):
                trace_e(start, marks + start).wait_recv()
            loop(1 - far, 1, passed_e)
            answer(recv_e, 5, FREE + 1, 5)
            from_below(5, 6)
            with scope("wait_h"):
                loop(odd, 1, passed_h)
            for t in range(TILES):
                here = pl.ds(8 * t, 8)
                own = be[2, here]
                e[2, at(1, t)] = e[2, at(1, t)] + own * (h[1, at(2, t)] + recv_h[start, 1, here])
                e[2, at(2, t)] = e[2, at(2, t)] - own * (h[1, at(1, t)] + recv_h[start, 0, here])

        def true(i):
            step = start + i
            final = (i + 1) // size
            deep = 1 - i // 2
            wide = far * (i // 2) * (1 - i // 3)

            def true_h(x, nxt):
                h_pass(e, h, ah, bh, x, nxt, x, x)

            def true_e(x, prv):
                e_pass(e, h, j, p, q, ae, be, bm, x, x, prv, x, x)

            with later(*(edges_e(e, x) for x in (0, 1, 2, 5, 6, 7))):
                true_h(3, 4)
                true_h(4, 5)
            with later(edges_h(h, 3), edges_h(h, 4)):
                true_h(1, 2)
                true_h(2, 3)
            loop(final, 1, lambda _: true_h(0, 1))
            with later(edges_h(h, 0), edges_h(h, 1), edges_h(h, 2)):
                true_e(3, 2)
                true_e(4, 3)
            loop(final, 1, lambda _: true_e(1, 0))
            with scope("wait_e"):
                trace_e(step, marks + step).wait_recv()
            take(e, 6, recv_e, step)
            with later(edges_e(e, 3), edges_e(e, 4)):
                true_h(5, CROSS)
            loop(final, 1, lambda _: true_h(6, 7))

            def wide_h(_):
                true_h(7, ZERO_E)
                for t in range(TILES):
                    b = bh[THIRD, pl.ds(8 * t, 8)]
                    h[FREE, at(1, t)] = b * e[0, at(2, t)]
                    h[FREE, at(2, t)] = -b * e[0, at(1, t)]
                edges_h(h, 7)()

            loop(1 - wide, 1, wide_h)
            for store in (edges_h(h, 5), edges_h(h, 6)):
                store()
            true_e(5, 4)
            loop(final, 1, lambda _: true_e(6, 5))
            loop(1 - deep, 1, lambda _: from_below(6, 7))
            with scope("wait_h"):
                trace_h(step, marks + step).wait_recv()
            take(h, 1, recv_h, step)
            with later(edges_e(e, 5)):
                true_e(2, CROSS)
            loop(1 - deep, 1, lambda _: from_own(0, 0, 0))

            def wide_e(_):
                true_e(7, 6)
                true_e(0, FREE)

            loop(1 - wide, 1, wide_e)

        with scope("ghostcoef"):
            loop((b + 3) // 4, 1, lambda _: arrive(be.at[pl.ds(0, 2)], x_sem.at[2]))

        with scope("true"):
            loop(1, size, true)

        def onward(_):
            give_e(OWN, start + size, 5 * lax.rem(b + 1, 2))
            h_part(OWN, OWN, start + size, 5 * lax.rem(b + 1, 2))

        loop(b // 2, 1, onward)
        return carry

    lax.fori_loop(0, BLOCKS, block, 0)

    with scope("finish"):
        arrive(send_e, s_sem.at[0])
        arrive(send_h, s_sem.at[1])
        arrive(raw.at[pl.ds(0, 5)], x_sem.at[3])
        rows = sum(BELOW[:4]) + sum(ABOVE[:4]) + (BELOW[4] + ABOVE[4]) // 2
        arrive(turned.at[0, :, pl.ds(0, rows)], y_sem.at[GROUPS])

    results = [(e, c) for c in range(3)] + [(h, c) for c in range(3)]
    outs = [(e_out, c) for c in range(3)] + [(h_out, c) for c in range(3)]
    with scope("results"):
        def gather(t):
            for g in range(2):
                group = results[4 * g : 4 * g + 4]
                tiles = [ref[OWN + x, pl.ds(pl.multiple_of(COMP * c + TILE * (t + 1), 8), 8)] for ref, c in group for x in range(4)]
                tiles = jnp.concatenate(tiles, 0)
                if g == 1:
                    tiles = jnp.concatenate([tiles, pltpu.roll(tiles, 64, 1)], 0)[:, :64]
                whole = jnp.transpose(tiles)
                for zb in range(8 if g == 0 else 4):
                    turned[g, zb, pl.ds(t, 16, stride=10)] = whole[16 * zb : 16 * zb + 16]

        loop_by(2, TILES, gather)

        def spread(g, zb):
            whole = jnp.transpose(turned[g, zb, pl.ds(16, 128)])
            group = outs[4 * g : 4 * g + 4]
            row = 0
            for block in (zb,) if g == 0 else (zb, zb + 4):
                for out, c in group:
                    for x in range(4):
                        out[c, block, pl.ds(x, 8, stride=4)] = whole[row : row + 8]
                        row += 8

        loop(0, 4, lambda zb: (spread(0, 2 * zb), spread(0, 2 * zb + 1), spread(1, zb)))


def hand_out(e, h, e_out, h_out, sem):
    copies = [
        pltpu.make_async_copy(ref.at[c], out.at[c], sem.at[3 * i + c])
        for i, (ref, out) in enumerate(((e, e_out), (h, h_out)))
        for c in range(3)
    ]
    for copy in copies:
        copy.start()
    for copy in copies:
        copy.wait()


def shards(
    e_field, h_field, drude_current, lorentz_polar, lorentz_rate, permittivity, material, absorber
):
    fields = [f.reshape(3, 8, 32, 128) for f in (e_field, h_field, drude_current, lorentz_polar, lorentz_rate)]
    cells = [c.reshape(8, 32, 128) for c in (permittivity, material, absorber)]
    wide = pltpu.VMEM((PLANES, 3 * COMP, 128), F32)
    narrow = pltpu.VMEM((PLANES, 3 * ROWS, 128), F32)
    cell = pltpu.VMEM((9, ROWS, 128), F32)
    trace = pltpu.VMEM((STEPS, 2, ROWS, 128), F32)
    e, h = pl.pallas_call(
        kernel,
        out_shape=(pltpu.VMEM((3, 8, 32, 128), F32),) * 2,
        in_specs=[pl.BlockSpec(memory_space=pl.ANY)] * 8,
        out_specs=(pl.BlockSpec(memory_space=pltpu.VMEM),) * 2,
        scratch_shapes=[
            pltpu.VMEM((18, 8, 32, 128), F32),
            pltpu.VMEM((2, 8, 32, 128), jnp.int32),
            pltpu.VMEM((GROUPS, 8, 160, 128), F32),
            pltpu.VMEM((8, 3, ROWS, 128), F32),
            wide, wide, narrow, narrow, narrow,
            cell, cell, cell, cell, cell, pltpu.VMEM((ROWS, 128), F32),
            trace, trace, trace, trace,
            pltpu.SemaphoreType.DMA((5,)),
            pltpu.SemaphoreType.DMA((GROUPS + 1,)),
            pltpu.SemaphoreType.DMA((5,)),
            pltpu.SemaphoreType.DMA((2,)),
            pltpu.SemaphoreType.DMA((10,)),
            pltpu.SemaphoreType.DMA((10,)),
        ],
        compiler_params=pltpu.CompilerParams(
            collective_id=0, has_side_effects=True, vmem_limit_bytes=48 * 1024 * 1024
        ),
    )(*(pltpu.with_memory_space_constraint(a, pltpu.HBM) for a in (*fields, *cells)))
    e, h = pl.pallas_call(
        hand_out,
        out_shape=(jax.ShapeDtypeStruct((3, 8, 32, 128), F32),) * 2,
        in_specs=[pl.BlockSpec(memory_space=pltpu.VMEM)] * 2,
        out_specs=(pl.BlockSpec(memory_space=pltpu.HBM),) * 2,
        scratch_shapes=[pltpu.SemaphoreType.DMA((6,))],
    )(*(pltpu.with_memory_space_constraint(a, pltpu.VMEM) for a in (e, h)))
    return e.reshape(3, 64, 4, 128), h.reshape(3, 64, 4, 128)


def solution(mesh):
    field, cell = P(None, None, "gx", "gy"), P(None, "gx", "gy")
    return jax.shard_map(
        shards, mesh=mesh, in_specs=(field,) * 5 + (cell,) * 3, out_specs=(field, field), check_vma=False
    )
```
